256 devices in a mesh: row: 8 (over y, z_hi), col: 32 (over z_lo, x, core).
Axes of the slice: x: 4, y: 4, z: 8 (z_hi: 2, z_lo: 4; z = z_hi * 4 + z_lo), core: 2. Of those that a mesh axis runs over, the one named last changes fastest.
Arguments:
- region: bfloat16 [128, 1536, 96], P('row', 'col'), may hold values from -6 to 6
- cotangent: bfloat16 [128, 1536, 96], P('row', 'col'), may hold values from -6 to 6
- norm_gains: float32 [2, 2, 96], replicated, may hold values from 0.5 to 1.5
- qkv_weight: bfloat16 [2, 96, 288], replicated, may hold values from -0.625 to 0.625
- qkv_bias: float32 [2, 288], replicated, may hold values from -3 to 3
- bias_table: float32 [2, 3, 225], replicated, may hold values from -4 to 300
- proj_weight: bfloat16 [2, 96, 96], replicated, may hold values from -0.625 to 0.625
- up_weight: bfloat16 [2, 96, 384], replicated, may hold values from -0.625 to 0.625
- up_bias: float32 [2, 384], replicated, may hold values from -3 to 3
- down_weight: bfloat16 [2, 384, 96], replicated, may hold values from -0.3125 to 0.3125
Outputs:
- output: bfloat16 [128, 1536, 96], P('row', 'col')
- grad_region: float32 [128, 1536, 96], P('row', 'col')
- grad_gains: float32 [2, 2, 96], replicated
- grad_qkv_weight: float32 [2, 96, 288], replicated
- grad_qkv_bias: float32 [2, 288], replicated
- grad_table: float32 [2, 3, 225], replicated
- grad_proj: float32 [2, 96, 96], replicated
- grad_up_weight: float32 [2, 96, 384], replicated
- grad_up_bias: float32 [2, 384], replicated
- grad_down_weight: float32 [2, 384, 96], replicated
The draws below stay inside these ranges and needn't reach their ends.
All inputs are finite; a program needn't handle non-finite values.
Results may differ from the reference program's by a relative error of at most 0.025.
Values may be sent and summed in bfloat16 or wider, within the bound.
No kernel may reach another device: no remote copies, remote signals or barrier semaphores. Data moves between devices by JAX's collectives and lax.ppermute only.
A program may use at most 64 MiB of HBM per device.

```python
import jax
import jax.numpy as jnp
from jax import lax

C = 96
HEADS = 3
HID = 384
WIN = 8
TH = 16
TW = 48
TABLE = 225
ROWS = 128
COLS = 1536
N_ROW = 8
N_COL = 32


def draw_bias_table(key, part):
    key = jax.random.fold_in(key, 11)
    base_key = jax.random.fold_in(key, 0)
    return jnp.clip(jax.random.normal(base_key, (2, HEADS, TABLE), jnp.float32), -4.0, 4.0)


def levels(stream_key, shape, cuts, smallest, largest):
    def one(axis_at, parts):
        heights = jax.random.uniform(jax.random.fold_in(jax.random.fold_in(stream_key, 6), axis_at), (parts,), jnp.float32, smallest / len(cuts), largest / len(cuts))
        return jnp.repeat(jnp.exp(heights), shape[axis_at] // parts).reshape((-1,) + (1,) * (len(shape) - axis_at - 1))

    level = one(*cuts[0])
    for cut in cuts[1:]:
        level = level * one(*cut)
    return level


def gaussian(stream_key, shape, deviation, bound, shards=(), kind=jnp.bfloat16):
    entries = deviation * jax.random.normal(stream_key, shape, jnp.float32)
    if shards:
        entries = entries * levels(stream_key, shape, shards, -0.22, 0.18)
    return jnp.clip(entries, -bound, bound).astype(kind)


def setup_inputs(seed: int = 0) -> dict:
    streams_of = jax.random.split(jax.random.key(seed), 11)
    region = gaussian(streams_of[0], (ROWS, COLS, C), 1.0, 6.0, ((0, 8), (1, 32)))
    cotangent = gaussian(streams_of[1], (ROWS, COLS, C), 1.0, 6.0, ((0, 8), (1, 32)))
    norm_gains = jnp.clip(1.0 + 0.1 * jax.random.normal(streams_of[2], (2, 2, C), jnp.float32), 0.5, 1.5)
    qkv_weight = gaussian(streams_of[3], (2, C, 3 * C), C ** -0.5, 0.625)
    qkv_bias = gaussian(streams_of[4], (2, 3 * C), 0.5, 3.0, (), jnp.float32)
    bias_table = draw_bias_table(jax.random.fold_in(streams_of[10], 71), 0)
    proj_weight = gaussian(streams_of[6], (2, C, C), C ** -0.5, 0.625)
    up_weight = gaussian(streams_of[7], (2, C, HID), C ** -0.5, 0.625)
    up_bias = gaussian(streams_of[8], (2, HID), 0.5, 3.0, (), jnp.float32)
    down_weight = gaussian(streams_of[9], (2, HID, C), HID ** -0.5, 0.3125)
    return dict(region=region, cotangent=cotangent, norm_gains=norm_gains, qkv_weight=qkv_weight, qkv_bias=qkv_bias, bias_table=bias_table, proj_weight=proj_weight, up_weight=up_weight, up_bias=up_bias, down_weight=down_weight)


HIGHEST = lax.Precision.HIGHEST

def layer_norm(values, gain):
    average = lax.optimization_barrier(jnp.mean(values, -1, keepdims=True))
    centred = values - average
    variance = lax.optimization_barrier(jnp.mean(centred * centred, -1, keepdims=True))
    return centred * lax.rsqrt(variance + 1e-05) * gain

def position_bias(table):
    positions = jnp.arange(WIN * WIN, dtype=jnp.int32)
    pos_row = positions // WIN
    pos_col = positions % WIN
    table_side = 2 * WIN - 1
    table_index = (pos_row[:, None] - pos_row[None, :] + WIN - 1) * table_side + (pos_col[:, None] - pos_col[None, :] + WIN - 1)
    onehot = (table_index[:, :, None] == jnp.arange(table_side * table_side, dtype=jnp.int32)[None, None, :]).astype(jnp.float32)
    return jnp.einsum('qkt,ht->hqk', onehot, table, precision=HIGHEST)

def windowize(field):
    height, width, depth = field.shape
    blocks = field.reshape(height // WIN, WIN, width // WIN, WIN, depth)
    return blocks.transpose(0, 2, 1, 3, 4).reshape(-1, WIN * WIN, depth)

def unwindowize(windows, height, width):
    depth = windows.shape[-1]
    blocks = windows.reshape(height // WIN, width // WIN, WIN, WIN, depth)
    return blocks.transpose(0, 2, 1, 3, 4).reshape(height, width, depth)

def attend(windows, usable, layer):
    gain_pair, qkv_weight, qkv_bias, table, proj_weight = layer[:5]
    win_count, win_tokens, channels = windows.shape
    head_count = table.shape[0]
    head_size = channels // head_count
    normed = layer_norm(windows, gain_pair[0]).astype(jnp.bfloat16).reshape(win_count * win_tokens, channels)
    triple = (jnp.dot(normed, qkv_weight, preferred_element_type=jnp.float32) + qkv_bias).astype(jnp.bfloat16)
    triple = triple.reshape(win_count, win_tokens, 3, head_count, head_size)
    queries = triple[:, :, 0].astype(jnp.float32)
    key_part = triple[:, :, 1].astype(jnp.float32)
    value_part = triple[:, :, 2].astype(jnp.float32)
    scores = jnp.einsum('wqhd,wkhd->whqk', queries, key_part) * head_size ** (-0.5) + position_bias(table)[None]
    if usable is not None:
        scores = jnp.where(usable[:, None, None, :], scores, -1e+30)
    highest = lax.stop_gradient(lax.optimization_barrier(jnp.max(scores, -1, keepdims=True)))
    exponent = jnp.exp(scores - highest)
    softmax_w = (exponent / lax.optimization_barrier(jnp.sum(exponent, -1, keepdims=True))).astype(jnp.bfloat16)
    mixture = jnp.einsum('whqk,wkhd->wqhd', softmax_w.astype(jnp.float32), value_part).astype(jnp.bfloat16)
    mixture = mixture.reshape(win_count * win_tokens, channels)
    projected = jnp.dot(mixture, proj_weight, preferred_element_type=jnp.float32)
    return windows + projected.reshape(win_count, win_tokens, channels)

def feed(field, layer):
    gain_pair = layer[0]
    up_weight, up_bias, down_weight = layer[5:]
    channels = field.shape[-1]
    flat_rows = field.reshape(-1, channels)
    normed = layer_norm(flat_rows, gain_pair[1]).astype(jnp.bfloat16)
    hidden = jax.nn.gelu(jnp.dot(normed, up_weight, preferred_element_type=jnp.float32) + up_bias).astype(jnp.bfloat16)
    return (flat_rows + jnp.dot(hidden, down_weight, preferred_element_type=jnp.float32)).reshape(field.shape)

def regular(field, layer):
    height, width, _ = field.shape
    return feed(unwindowize(attend(windowize(field), None, layer), height, width), layer)

def shifted(padded, row_start, col_start, total_rows, total_cols, layer):
    half_win = WIN // 2
    height = padded.shape[0] - WIN
    width = padded.shape[1] - WIN
    row_ids = row_start + jnp.arange(height + WIN, dtype=jnp.int32)
    col_ids = col_start + jnp.arange(width + WIN, dtype=jnp.int32)
    inside = ((row_ids >= 0) & (row_ids < total_rows))[:, None] & ((col_ids >= 0) & (col_ids < total_cols))[None, :]
    usable = windowize(inside[:, :, None]).reshape(-1, WIN * WIN)
    mixed_field = unwindowize(attend(windowize(padded), usable, layer), height + WIN, width + WIN)
    return feed(mixed_field[half_win:half_win + height, half_win:half_win + width], layer)

def to_tiles(field):
    depth = field.shape[-1]
    return field.reshape(N_ROW, TH, N_COL, TW, depth).transpose(0, 2, 1, 3, 4).reshape(N_ROW * N_COL, TH, TW, depth)

def from_tiles(tiles):
    depth = tiles.shape[-1]
    return tiles.reshape(N_ROW, N_COL, TH, TW, depth).transpose(0, 2, 1, 3, 4).reshape(ROWS, COLS, depth)

def reference(region, cotangent, norm_gains, qkv_weight, qkv_bias, bias_table, proj_weight, up_weight, up_bias, down_weight):
    stacked = (norm_gains, qkv_weight, qkv_bias, bias_table, proj_weight, up_weight, up_bias, down_weight)
    lower_layer = tuple((entry[0] for entry in stacked))
    upper_layer = tuple((entry[1] for entry in stacked))
    half_win = WIN // 2
    region_tiles = to_tiles(region)
    cot_tiles = to_tiles(cotangent)
    lower_tiles = lax.map(lambda tile_in: regular(tile_in.astype(jnp.float32), lower_layer).astype(jnp.bfloat16), region_tiles)
    padded = jnp.pad(from_tiles(lower_tiles), ((half_win, half_win), (half_win, half_win), (0, 0)))
    zero_sums = tuple((jnp.zeros(entry.shape, jnp.float32) for entry in upper_layer))

    def upper_step(state_pair, number):
        grad_field, totals = state_pair
        tile_row = number // N_COL
        tile_col = number % N_COL
        starts = ((tile_row * TH).astype(jnp.int32), (tile_col * TW).astype(jnp.int32), jnp.zeros((), jnp.int32))
        patch = lax.dynamic_slice(padded, starts, (TH + WIN, TW + WIN, C)).astype(jnp.float32)

        def upper_block(field, layer):
            return shifted(field, tile_row * TH - half_win, tile_col * TW - half_win, ROWS, COLS, layer)
        result, pull_upper = jax.vjp(upper_block, patch, upper_layer)
        grad_patch, grad_layer = pull_upper(cot_tiles[number].astype(jnp.float32))
        current = lax.dynamic_slice(grad_field, starts, grad_patch.shape)
        grad_field = lax.dynamic_update_slice(grad_field, current + grad_patch, starts)
        totals = tuple((total + part.astype(jnp.float32) for total, part in zip(totals, grad_layer)))
        return ((grad_field, totals), result.astype(jnp.bfloat16))
    start_field = jnp.zeros((ROWS + WIN, COLS + WIN, C), jnp.float32)
    (grad_field, upper_totals), upper_tiles = lax.scan(upper_step, (start_field, zero_sums), jnp.arange(N_ROW * N_COL, dtype=jnp.int32))
    grad_lower = grad_field[half_win:half_win + ROWS, half_win:half_win + COLS]

    def lower_step(totals, pair):
        tile_in, tile_grad = pair
        _, pull_lower = jax.vjp(regular, tile_in.astype(jnp.float32), lower_layer)
        grad_tile, grad_layer = pull_lower(tile_grad)
        totals = tuple((total + part.astype(jnp.float32) for total, part in zip(totals, grad_layer)))
        return (totals, grad_tile)
    lower_totals, grad_tiles = lax.scan(lower_step, zero_sums, (region_tiles, to_tiles(grad_lower)))
    grads = [jnp.stack([low_part, up_part]) for low_part, up_part in zip(lower_totals, upper_totals)]
    return (from_tiles(upper_tiles), from_tiles(grad_tiles), grads[0], grads[1], grads[2], grads[3], grads[4], grads[5], grads[6], grads[7])
```

```python
import jax
import jax.numpy as jnp
from jax import lax
from jax.experimental import pallas as pl
from jax.experimental.pallas import tpu as pltpu
from jax.sharding import Mesh
from jax.sharding import PartitionSpec as P

C = 96
HEADS = 3
HEAD = 32
HID = 384
WIN = 8
TH = 16
TW = 48
AUG = 112
PAIR = 128
ROWS = 1024
PEERS = 128
GROUP = 256
LOG2E = 1.4426950408889634
SCALE = HEAD**-0.5
FAR = -1e30
F32 = jnp.float32
BF16 = jnp.bfloat16

LOWER = [(i, j) for i in (1, 2) for j in range(1, 7)]
LOWER += [(i, j) for i in range(4) for j in range(8) if (i, j) not in LOWER]
UPPER = [(i, j) for i in (0, 1) for j in range(6)]
UPPER += [(2, j) for j in range(7)] + [(0, 6), (1, 6)]
LOWER_GROUPS = 8
OWN_GROUPS = 3
UPPER_GROUPS = 6


def dot(a, b):
    return jnp.dot(a, b, preferred_element_type=F32)


def dot_nt(a, b):
    return lax.dot_general(a, b, (((1,), (1,)), ((), ())), preferred_element_type=F32)


def split3(v):
    hi = v.astype(BF16)
    rest = v - hi.astype(F32)
    mid = rest.astype(BF16)
    return hi, mid, (rest - mid.astype(F32)).astype(BF16)


def transposed(v):
    return jnp.transpose(v.astype(F32)).astype(BF16)


def augmented(weight, bias):
    hi, mid, lo = split3(bias)
    rows = lax.broadcasted_iota(jnp.int32, (AUG - C, bias.shape[1]), 0)
    extra = jnp.where(
        rows == 0,
        hi.astype(F32),
        jnp.where(rows == 1, mid.astype(F32), jnp.where(rows == 2, lo.astype(F32), 0.0)),
    )
    return transposed(jnp.concatenate([weight.astype(F32), extra], 0))


def lane_code(lanes):
    token = lanes % 64
    return (token // WIN) * 15 + token % WIN


def expand_table(row):
    parts = []
    for kr in range(WIN):
        wide = jnp.broadcast_to(row, (WIN, 256))
        parts.append(pltpu.roll(wide, (15 * kr - 112) % 256, 1, stride=1, stride_axis=0))
    rolled = jnp.concatenate(parts, 0)
    lane = lax.broadcasted_iota(jnp.int32, (256, PAIR), 0)
    query = lax.broadcasted_iota(jnp.int32, (256, PAIR), 1)
    onehot = (lane == lane_code(query)).astype(BF16)
    hi, mid, lo = split3(rolled)
    both = dot(hi, onehot) + dot(mid, onehot) + dot(lo, onehot)
    first = lax.broadcasted_iota(jnp.int32, both.shape, 1) < 64
    return jnp.concatenate([jnp.where(first, both, FAR), jnp.where(first, FAR, both)], 0) * LOG2E


def fold_table(acc):
    both = acc[:64] + acc[64:]
    lane = lax.broadcasted_iota(jnp.int32, (PAIR, 256), 1)
    query = lax.broadcasted_iota(jnp.int32, (PAIR, 256), 0)
    onehot = (lane == 112 - lane_code(query)).astype(BF16)
    hi, mid, _ = split3(both)
    wide = dot(hi, onehot) + dot(mid, onehot)
    total = jnp.zeros((WIN, 256), F32)
    for kr in range(WIN):
        total += pltpu.roll(
            wide[kr * WIN : (kr + 1) * WIN], 15 * kr, 1, stride=1, stride_axis=0
        )
    return jnp.sum(total, 0, keepdims=True)


def reverse_lanes(rows):
    a = lax.broadcasted_iota(jnp.int32, (256, 256), 0)
    b = lax.broadcasted_iota(jnp.int32, (256, 256), 1)
    onehot = (a + b == 224).astype(BF16)
    hi, mid, _ = split3(rows)
    return dot(hi, onehot) + dot(mid, onehot)


def norm(x):
    mean = jnp.sum(x, 0, keepdims=True) * (1.0 / C)
    centred = x - mean
    var = jnp.sum(centred * centred, 0, keepdims=True) * (1.0 / C)
    r = lax.rsqrt(var + 1e-05)
    return centred * r, r


def norm_back(dxhat, xhat, r):
    m1 = jnp.sum(dxhat, 0, keepdims=True) * (1.0 / C)
    m2 = jnp.sum(dxhat * xhat, 0, keepdims=True) * (1.0 / C)
    return r * (dxhat - m1 - xhat * m2)


def wide_gain(gain):
    return jnp.concatenate([gain] * (GROUP // PAIR), 1)


def with_ones(v):
    return jnp.concatenate([v, jnp.ones((AUG - C, v.shape[1]), BF16)], 0)


def head_blocks(v):
    zero = jnp.zeros((HEAD, PAIR), v.dtype)
    cols = []
    for h in range(HEADS):
        rows = [v[g * HEAD : (g + 1) * HEAD] if g == h else zero for g in range(HEADS)]
        cols.append(jnp.concatenate(rows, 0))
    return jnp.concatenate(cols, 1)


def head_diagonal(v):
    return jnp.concatenate(
        [v[h * HEAD : (h + 1) * HEAD, h * PAIR : (h + 1) * PAIR] for h in range(HEADS)], 0
    )


def gelu_parts(u):
    k = 0.7978845608028654
    uu = u * u
    t = jnp.tanh(u * (k + (k * 0.044715) * uu))
    half = 0.5 + 0.5 * t
    slope = half + (half * (1.0 - t)) * u * (k + (3 * k * 0.044715) * uu)
    return u * half, slope


def forward(x, b, w, penalty):
    xhat1, r1 = norm(x)
    a = with_ones((xhat1 * wide_gain(w.gain[b, 0])).astype(BF16))
    qkv = dot(w.qkv_t[b], a).astype(BF16)
    probs, mixed, tokens = [], [], []
    for p in range(2):
        lanes = slice(p * PAIR, (p + 1) * PAIR)
        key_tok = transposed(qkv[C : 2 * C, lanes])
        scores = dot(key_tok, head_blocks(qkv[:C, lanes])) * (SCALE * LOG2E) + w.bias[b]
        if penalty is not None:
            scores = scores + jnp.concatenate([penalty[p]] * HEADS, 1)
        e = jnp.exp2(scores - jnp.max(scores, 0, keepdims=True))
        prob = (e * (1.0 / jnp.sum(e, 0, keepdims=True))).astype(BF16)
        mixed.append(head_diagonal(dot(qkv[2 * C :, lanes], prob)))
        probs.append(prob)
    mix = jnp.concatenate(mixed, 1).astype(BF16)
    h = x + dot(w.proj_t[b], mix)
    xhat2, r2 = norm(h)
    f = with_ones((xhat2 * wide_gain(w.gain[b, 1])).astype(BF16))
    u = dot(w.up_t[b], f)
    m, slope = gelu_parts(u)
    m = m.astype(BF16)
    out = h + dot(w.down_t[b], m)
    return out, (xhat1, r1, a, qkv, probs, mix, xhat2, r2, f, m, slope)


def backward(g, b, w, saved, mask):
    xhat1, r1, a, qkv, probs, mix, xhat2, r2, f, m, slope = saved

    def own(v):
        return v if mask is None else v * mask.astype(v.dtype)

    def own_pair(v, p):
        if mask is None:
            return v
        return v * jnp.concatenate([mask[:, p * PAIR : (p + 1) * PAIR]] * HEADS, 1)

    def lanes_sum(v):
        return v[:, :PAIR] + v[:, PAIR:]

    g16 = g.astype(BF16)
    du = (dot(w.down[b], g16) * slope).astype(BF16)
    w.d_down[b] += dot_nt(own(g16), m)
    w.d_up[b] += dot_nt(own(f), du)
    df = dot(w.up[b], du)
    w.d_gain[b, 1] += lanes_sum(own(df * xhat2))
    dh = g + norm_back(df * wide_gain(w.gain[b, 1]), xhat2, r2)
    dh16 = dh.astype(BF16)
    w.d_proj[b] += dot_nt(mix, own(dh16))
    dmix = dot(w.proj[b], dh16).astype(BF16)
    dq, dk, dv = [], [], []
    for p in range(2):
        lanes = slice(p * PAIR, (p + 1) * PAIR)
        val_tok = transposed(qkv[2 * C :, lanes])
        blocks = head_blocks(dmix[:, lanes])
        dprob = dot(val_tok, blocks)
        prob = probs[p].astype(F32)
        weighted = prob * dprob
        ds = weighted - prob * jnp.sum(weighted, 0, keepdims=True)
        w.d_bias[b] += own_pair(ds, p)
        ds16 = ds.astype(BF16)
        dv.append(dot_nt(blocks, probs[p]))
        dk.append(dot_nt(head_blocks(qkv[:C, lanes]), ds16) * SCALE)
        dq.append(head_diagonal(dot(qkv[C : 2 * C, lanes], ds16)) * SCALE)
    dqkv = jnp.concatenate([jnp.concatenate(v, 1) for v in (dq, dk, dv)], 0).astype(BF16)
    w.d_qkv[b] += dot_nt(own(a), dqkv)
    da = dot(w.qkv[b], dqkv)
    w.d_gain[b, 0] += lanes_sum(own(da * xhat1))
    return dh + norm_back(da * wide_gain(w.gain[b, 0]), xhat1, r1)


class Layers:
    pass


def windows_t(ref, places, r0, c0):
    tokens = []
    for i, j in places:
        block = ref[r0 + WIN * i : r0 + WIN * (i + 1), c0 + WIN * j : c0 + WIN * (j + 1), :]
        tokens.append(block.astype(F32).reshape(WIN * WIN, C))
    if len(tokens) == 1:
        tokens.append(jnp.zeros((WIN * WIN, C), F32))
    return jnp.transpose(jnp.concatenate(tokens, 0))


def windows_back(value, ref, places):
    tokens = jnp.transpose(value)
    for n, (i, j) in enumerate(places):
        block = tokens[n * 64 : (n + 1) * 64].reshape(WIN, WIN, C)
        ref[WIN * i : WIN * (i + 1), WIN * j : WIN * (j + 1), :] = block.astype(ref.dtype)


def kernel(
    place,
    region,
    cot,
    row_a,
    row_b,
    col_a,
    col_b,
    norm_gains,
    qkv_weight,
    qkv_bias,
    bias_table,
    proj_weight,
    up_weight,
    up_bias,
    down_t,
    out,
    grad_region,
    packed,
    wide_region,
    wide_cot,
    x_low,
    y_low,
    x_up,
    g_up,
    y_up,
    dx_up,
    low_field,
    out_field,
    grad_field,
    table,
    misc,
    gain,
    qkv_t,
    proj_t,
    up_t,
    down,
    bias,
    d_gain,
    d_qkv,
    d_proj,
    d_up,
    d_down,
    d_bias,
    *saves,
):
    w = Layers()
    w.qkv, w.proj, w.up, w.down_t = qkv_weight, proj_weight, up_weight, down_t
    w.gain, w.qkv_t, w.proj_t, w.up_t, w.down, w.bias = gain, qkv_t, proj_t, up_t, down, bias
    w.d_gain, w.d_qkv, w.d_proj = d_gain, d_qkv, d_proj
    w.d_up, w.d_down, w.d_bias = d_up, d_down, d_bias
    s_prob = saves[4]
    first_row, last_row = place[0] == 0, place[0] == place[2] - 1
    first_col, last_col = place[1] == 0, place[1] == place[3] - 1

    above, below = sides(place[0], row_a[...], row_b[...])
    left, right = sides(place[1], col_a[...], col_b[...])
    inner = slice(8, 8 + TW)
    wide_region[0:8, inner, :] = above[0:8].astype(F32)
    wide_region[8:24, inner, :] = region[...].astype(F32)
    wide_region[24:32, inner, :] = below[0:8].astype(F32)
    wide_region[:, 0:8, :] = left[0:32].astype(F32)
    wide_region[:, 8 + TW :, :] = right[0:32].astype(F32)
    wide_cot[0:4, inner, :] = above[8:12].astype(F32)
    wide_cot[4:20, inner, :] = cot[...].astype(F32)
    wide_cot[20:24, inner, :] = below[8:12].astype(F32)
    wide_cot[:, 0:8, :] = left[32:56].astype(F32)
    wide_cot[:, 8 + TW :, :] = right[32:56].astype(F32)

    for ref in (d_gain, d_qkv, d_proj, d_up, d_down, d_bias, table, misc):
        ref[...] = jnp.zeros(ref.shape, F32)
    for b in range(2):
        qkv_t[b] = augmented(qkv_weight[b], qkv_bias[b : b + 1, :])
        up_t[b] = augmented(up_weight[b], up_bias[b : b + 1, :])
        proj_t[b] = transposed(proj_weight[b])
        down[b] = transposed(down_t[b])
        for n in range(2):
            row = jnp.broadcast_to(norm_gains[b, n : n + 1, :], (PAIR, C))
            gain[b, n] = jnp.transpose(row)
        for h in range(HEADS):
            table[b, h : h + 1, 0 : bias_table.shape[2]] = bias_table[h, b : b + 1, :]
            bias[b, :, h * PAIR : (h + 1) * PAIR] = expand_table(table[b, h : h + 1, :])

    for n in range(2 * LOWER_GROUPS):
        value = windows_t(wide_region, LOWER[2 * n : 2 * n + 2], 0, 0)
        x_low[n // 2, :, (n % 2) * PAIR : (n % 2 + 1) * PAIR] = value

    def own_step(g, _):
        y, saved = forward(x_low[g], 0, w, None)
        y_low[g] = y.astype(BF16).astype(F32)
        for ref, value in zip(saves, saved):
            if ref is s_prob:
                for p in range(2):
                    ref[g, p] = value[p]
            else:
                ref[g] = value
        return 0

    lax.fori_loop(0, OWN_GROUPS, own_step, 0)

    def halo_step(g, _):
        y, _ = forward(x_low[g], 0, w, None)
        y_low[g] = y.astype(BF16).astype(F32)
        return 0

    lax.fori_loop(OWN_GROUPS, LOWER_GROUPS, halo_step, 0)

    for n in range(2 * LOWER_GROUPS):
        value = y_low[n // 2, :, (n % 2) * PAIR : (n % 2 + 1) * PAIR]
        windows_back(value, low_field, LOWER[2 * n : 2 * n + 2])

    for n in range(2 * UPPER_GROUPS):
        lanes = slice((n % 2) * PAIR, (n % 2 + 1) * PAIR)
        places = UPPER[2 * n : 2 * n + 2]
        if places:
            x_up[n // 2, :, lanes] = windows_t(low_field, places, 4, 4)
            g_up[n // 2, :, lanes] = windows_t(wide_cot, places, 0, 4)
        else:
            x_up[n // 2, :, lanes] = jnp.zeros((C, PAIR), F32)
            g_up[n // 2, :, lanes] = jnp.zeros((C, PAIR), F32)

    def edges(s):
        top = first_row & ((s < 6) | (s == 19))
        bottom = last_row & (s >= 12) & (s < 19)
        left = first_col & ((s == 0) | (s == 6) | (s == 12))
        right = last_col & (s >= 18) & (s < 21)
        return [jnp.where(v, FAR, 0.0) for v in (top, bottom, left, right)]

    def upper_step(g, _):
        key = lax.broadcasted_iota(jnp.int32, (PAIR, PAIR), 0)
        upper_half = ((key // WIN) % WIN) < 4
        left_half = (key % WIN) < 4
        penalty = []
        for p in range(2):
            one, two = edges(4 * g + 2 * p), edges(4 * g + 2 * p + 1)
            top, bottom, left, right = [jnp.where(key < 64, v, u) for v, u in zip(one, two)]
            penalty.append(
                jnp.where(upper_half, top, bottom) + jnp.where(left_half, left, right)
            )
        slot = 4 * g + lax.broadcasted_iota(jnp.int32, (1, GROUP), 1) // 64
        row_own = jnp.where(last_row, 1.0, 0.0)
        col_own = jnp.where(last_col, 1.0, 0.0)
        mask = jnp.where(
            slot < 12,
            1.0,
            jnp.where(
                slot < 18,
                row_own,
                jnp.where(slot < 19, row_own * col_own, jnp.where(slot < 21, col_own, 0.0)),
            ),
        )
        y, saved = forward(x_up[g], 1, w, penalty)
        y_up[g] = y
        dx_up[g] = backward(g_up[g], 1, w, saved, mask)
        return 0

    lax.fori_loop(0, UPPER_GROUPS, upper_step, 0)

    for n in range(2 * UPPER_GROUPS):
        lanes = slice((n % 2) * PAIR, (n % 2 + 1) * PAIR)
        places = UPPER[2 * n : 2 * n + 2]
        if places:
            windows_back(y_up[n // 2, :, lanes], out_field, places)
            windows_back(dx_up[n // 2, :, lanes], grad_field, places)
    out[...] = out_field[4 : 4 + TH, 4 : 4 + TW, :].astype(BF16)

    for n in range(2 * OWN_GROUPS):
        lanes = slice((n % 2) * PAIR, (n % 2 + 1) * PAIR)
        g_up[n // 2, :, lanes] = windows_t(grad_field, UPPER[2 * n : 2 * n + 2], 4, 4)

    def lower_step(g, _):
        saved = [[ref[g, 0], ref[g, 1]] if ref is s_prob else ref[g] for ref in saves]
        dx_up[g] = backward(g_up[g], 0, w, saved, None)
        return 0

    lax.fori_loop(0, OWN_GROUPS, lower_step, 0)

    for n in range(2 * OWN_GROUPS):
        lanes = slice((n % 2) * PAIR, (n % 2 + 1) * PAIR)
        windows_back(dx_up[n // 2, :, lanes], grad_region, UPPER[2 * n : 2 * n + 2])

    for b in range(2):
        for j in range(3):
            lanes = slice(j * PAIR, (j + 1) * PAIR)
            packed[b, j * C : (j + 1) * C, :] = d_up[b, 0:C, lanes].astype(BF16)
            packed[b, 288 + j * C : 288 + (j + 1) * C, :] = d_down[b, :, lanes].astype(BF16)
            misc[b, 3 + j : 4 + j, :] = d_up[b, C : C + 1, lanes]
        for j in range(2):
            lanes = slice(j * PAIR, (j + 1) * PAIR)
            packed[b, 576 + j * C : 576 + (j + 1) * C, :] = d_qkv[b, 0:C, lanes].astype(BF16)
            misc[b, j : j + 1, :] = d_qkv[b, C : C + 1, lanes]
        last = jnp.concatenate([d_qkv[b, 0:C, 256:288], d_proj[b]], 1)
        packed[b, 768:864, :] = last.astype(BF16)
        misc[b, 2:3, 0:32] = d_qkv[b, C : C + 1, 256:288]
        for n in range(2):
            column = jnp.sum(jnp.transpose(d_gain[b, n]), 0, keepdims=True)
            misc[b, 6 + n : 7 + n, 0:C] = column
        for h in range(HEADS):
            table[b, h : h + 1, :] = fold_table(d_bias[b, :, h * PAIR : (h + 1) * PAIR])
        rows = reverse_lanes(table[b])
        misc[b, 8:16, :] = rows[:, 0:PAIR]
        misc[b, 16:24, :] = rows[:, PAIR:]
        packed[b, 864:896, :] = misc[b].astype(BF16)
        packed[b, 896:ROWS, :] = jnp.zeros((ROWS - 896, PAIR), BF16)


VMEM = pl.BlockSpec(memory_space=pltpu.VMEM)
SMEM = pl.BlockSpec(memory_space=pltpu.SMEM)


def local(place, arrays):
    shapes = [
        ((TH + 16, TW + 16, C), F32),
        ((TH + 8, TW + 16, C), F32),
        ((LOWER_GROUPS, C, GROUP), F32),
        ((LOWER_GROUPS, C, GROUP), F32),
        ((UPPER_GROUPS, C, GROUP), F32),
        ((UPPER_GROUPS, C, GROUP), F32),
        ((UPPER_GROUPS, C, GROUP), F32),
        ((UPPER_GROUPS, C, GROUP), F32),
        ((TH + 16, TW + 16, C), F32),
        ((TH + 8, TW + 8, C), F32),
        ((TH + 8, TW + 8, C), F32),
        ((2, 8, 256), F32),
        ((2, 32, PAIR), F32),
        ((2, 2, C, PAIR), F32),
        ((2, 3 * C, AUG), BF16),
        ((2, C, C), BF16),
        ((2, HID, AUG), BF16),
        ((2, HID, C), BF16),
        ((2, PAIR, HEADS * PAIR), F32),
        ((2, 2, C, PAIR), F32),
        ((2, AUG, 3 * C), F32),
        ((2, C, C), F32),
        ((2, AUG, HID), F32),
        ((2, C, HID), F32),
        ((2, PAIR, HEADS * PAIR), F32),
        ((OWN_GROUPS, C, GROUP), F32),
        ((OWN_GROUPS, 1, GROUP), F32),
        ((OWN_GROUPS, AUG, GROUP), BF16),
        ((OWN_GROUPS, 3 * C, GROUP), BF16),
        ((OWN_GROUPS, 2, PAIR, HEADS * PAIR), BF16),
        ((OWN_GROUPS, C, GROUP), BF16),
        ((OWN_GROUPS, C, GROUP), F32),
        ((OWN_GROUPS, 1, GROUP), F32),
        ((OWN_GROUPS, AUG, GROUP), BF16),
        ((OWN_GROUPS, HID, GROUP), BF16),
        ((OWN_GROUPS, HID, GROUP), F32),
    ]
    return pl.pallas_call(
        kernel,
        out_shape=(
            jax.ShapeDtypeStruct((TH, TW, C), BF16),
            jax.ShapeDtypeStruct((TH, TW, C), F32),
            jax.ShapeDtypeStruct((2, ROWS, PAIR), BF16),
        ),
        in_specs=[SMEM] + [VMEM] * len(arrays),
        out_specs=[VMEM] * 3,
        scratch_shapes=[pltpu.VMEM(shape, kind) for shape, kind in shapes],
        compiler_params=pltpu.CompilerParams(vmem_limit_bytes=48 * 1024 * 1024),
        name="blocks",
    )(place, *arrays)


def sides(position, from_a, from_b):
    even = position % 2 == 0
    return jnp.where(even, from_b, from_a), jnp.where(even, from_a, from_b)


def row_kernel(place, region, cot, send_a, send_b):
    even = place[0] % 2 == 0
    for dst, top in ((send_a, jnp.logical_not(even)), (send_b, even)):
        dst[0:8] = jnp.where(top, region[0:8], region[8:16])
        dst[8:12] = jnp.where(top, cot[0:4], cot[12:16])


def col_kernel(place, region, cot, row_a, row_b, send_a, send_b):
    above, below = sides(place[0], row_a[...], row_b[...])
    even = place[1] % 2 == 0
    for dst, left in ((send_a, jnp.logical_not(even)), (send_b, even)):
        for rows, value in (
            (slice(0, 8), above[0:8]),
            (slice(8, 24), region[...]),
            (slice(24, 32), below[0:8]),
            (slice(32, 36), above[8:12]),
            (slice(36, 52), cot[...]),
            (slice(52, 56), below[8:12]),
        ):
            dst[rows] = jnp.where(left, value[:, 0:8], value[:, TW - 8 :])


def unpack_kernel(
    place, mine, other, gains, qkv, qkv_bias, table, proj, up, up_bias, down_t
):
    core = place[1] % 2
    for b in range(2):
        flat = jnp.where(core == b, mine[...], other[...]).astype(F32)
        misc = flat[864:896]
        for j in range(3):
            lanes = slice(j * PAIR, (j + 1) * PAIR)
            up[b, :, lanes] = flat[j * C : (j + 1) * C]
            down_t[b, :, lanes] = flat[288 + j * C : 288 + (j + 1) * C]
            up_bias[b : b + 1, lanes] = misc[3 + j : 4 + j]
        for j in range(2):
            lanes = slice(j * PAIR, (j + 1) * PAIR)
            qkv[b, :, lanes] = flat[576 + j * C : 576 + (j + 1) * C]
            qkv_bias[b : b + 1, lanes] = misc[j : j + 1]
        last = flat[768:864]
        qkv[b, :, 256:288] = last[:, 0:32]
        proj[b] = last[:, 32:PAIR]
        qkv_bias[b : b + 1, 256:288] = misc[2:3, 0:32]
        for n in range(2):
            gains[b, n : n + 1, :] = misc[6 + n : 7 + n, 0:C]
        for h in range(HEADS):
            table[h, b : b + 1, 0:PAIR] = misc[8 + h : 9 + h]
            table[h, b : b + 1, PAIR:225] = misc[16 + h : 17 + h, 0:97]


def near(count):
    return [(i, i ^ 1) for i in range(count)]


def far(count):
    return [(i, ((i - 1) ^ 1) + 1) for i in range(1, count - 1)]


def swap(pair, axes, count):
    return lax.ppermute(pair[0], axes, near(count)), lax.ppermute(pair[1], axes, far(count))


def body(region, cotangent, gains, qkv, qkv_bias, table, proj, up, up_bias, down):
    col_axes = ("col_half", "core")
    rows, cols = lax.axis_size("row"), lax.axis_size(col_axes)
    core = lax.axis_index("core")
    place = jnp.stack(
        [lax.axis_index("row"), lax.axis_index(col_axes), jnp.int32(rows), jnp.int32(cols)]
    ).astype(jnp.int32)
    strip = jax.ShapeDtypeStruct((12, TW, C), BF16)
    send = pl.pallas_call(
        row_kernel,
        out_shape=(strip, strip),
        in_specs=[SMEM, VMEM, VMEM],
        out_specs=[VMEM] * 2,
        name="row_strips",
    )(place, region, cotangent)
    row_got = swap(send, "row", rows)
    strip = jax.ShapeDtypeStruct((56, 8, C), BF16)
    send = pl.pallas_call(
        col_kernel,
        out_shape=(strip, strip),
        in_specs=[SMEM] + [VMEM] * 4,
        out_specs=[VMEM] * 2,
        name="col_strips",
    )(place, region, cotangent, *row_got)
    col_got = swap(send, col_axes, cols)
    table_t = jnp.transpose(table, (1, 0, 2))
    down_t = jnp.transpose(down, (0, 2, 1))
    out, grad_region, packed = local(
        place,
        (region, cotangent, *row_got, *col_got)
        + (gains, qkv, qkv_bias, table_t, proj, up, up_bias, down_t),
    )
    keep = lax.dynamic_index_in_dim(packed, core, 0, keepdims=False)
    give = lax.dynamic_index_in_dim(packed, 1 - core, 0, keepdims=False)
    got = lax.ppermute(give, "core", near(2))
    share = (keep.astype(F32) + got.astype(F32)).astype(BF16).reshape(PEERS, -1, PAIR)
    peers = ("row", "col_half")
    parts = lax.all_to_all(share, peers, 0, 0)
    part = jnp.sum(parts.astype(F32), 0, keepdims=True).astype(BF16)
    mine = lax.all_to_all(jnp.broadcast_to(part, share.shape), peers, 0, 0)
    mine = mine.reshape(ROWS, PAIR)
    other = lax.ppermute(mine, "core", near(2))
    grads = pl.pallas_call(
        unpack_kernel,
        out_shape=tuple(
            jax.ShapeDtypeStruct(shape, F32)
            for shape in (
                (2, 2, C),
                (2, C, 3 * C),
                (2, 3 * C),
                (HEADS, 2, 225),
                (2, C, C),
                (2, C, HID),
                (2, HID),
                (2, C, HID),
            )
        ),
        in_specs=[SMEM, VMEM, VMEM],
        out_specs=[VMEM] * 8,
        name="unpack",
    )(place, mine, other)
    d_gains, d_qkv, d_qkv_bias, d_table, d_proj, d_up, d_up_bias, d_down_t = grads
    return (
        out,
        grad_region,
        d_gains,
        d_qkv,
        d_qkv_bias,
        jnp.transpose(d_table, (1, 0, 2)),
        d_proj,
        d_up,
        d_up_bias,
        jnp.transpose(d_down_t, (0, 2, 1)),
    )


def solution(mesh):
    rows, cols = mesh.devices.shape
    fine = Mesh(mesh.devices.reshape(rows, cols // 2, 2), ("row", "col_half", "core"))
    tile = P("row", ("col_half", "core"), None)
    return jax.shard_map(
        body,
        mesh=fine,
        in_specs=(tile, tile) + (P(),) * 8,
        out_specs=(tile, tile) + (P(),) * 8,
        check_vma=False,
    )
```

```python
import functools

import jax
import jax.numpy as jnp
from jax import lax
from jax.experimental import pallas as pl
from jax.experimental.pallas import tpu as pltpu
from jax.sharding import Mesh
from jax.sharding import PartitionSpec as P

C = 96
HEADS = 3
HEAD = 32
HID = 384
WIN = 8
TH = 16
TW = 48
AUG = 112
PAIR = 128
ROWS = 1024
PEERS = 128
LOG2E = 1.4426950408889634
SCALE = HEAD**-0.5
FAR = -1e30
F32 = jnp.float32
BF16 = jnp.bfloat16

LOWER = [(i, j) for i in (0, 1) for j in range(6)]
UPPER = LOWER + [(2, j) for j in range(7)] + [(0, 6), (1, 6)]
OWN_PAIRS = 6
UPPER_PAIRS = 11
CHUNK = 2
LIMIT = 60 * 1024 * 1024


def dot(a, b):
    return jnp.dot(a, b, preferred_element_type=F32)


def dot_nt(a, b):
    return lax.dot_general(a, b, (((1,), (1,)), ((), ())), preferred_element_type=F32)


def split3(v):
    hi = v.astype(BF16)
    rest = v - hi.astype(F32)
    mid = rest.astype(BF16)
    return hi, mid, (rest - mid.astype(F32)).astype(BF16)


def transposed(v):
    return jnp.transpose(v.astype(F32)).astype(BF16)


def augmented(weight, bias):
    hi, mid, lo = split3(bias)
    rows = lax.broadcasted_iota(jnp.int32, (AUG - C, bias.shape[1]), 0)
    extra = jnp.where(
        rows == 0,
        hi.astype(F32),
        jnp.where(rows == 1, mid.astype(F32), jnp.where(rows == 2, lo.astype(F32), 0.0)),
    )
    return transposed(jnp.concatenate([weight.astype(F32), extra], 0))


def lane_code(lanes):
    token = lanes % 64
    return (token // WIN) * 15 + token % WIN


def expand_table(row):
    parts = []
    for kr in range(WIN):
        wide = jnp.broadcast_to(row, (WIN, 256))
        parts.append(pltpu.roll(wide, (15 * kr - 112) % 256, 1, stride=1, stride_axis=0))
    rolled = jnp.concatenate(parts, 0)
    lane = lax.broadcasted_iota(jnp.int32, (256, PAIR), 0)
    query = lax.broadcasted_iota(jnp.int32, (256, PAIR), 1)
    onehot = (lane == lane_code(query)).astype(BF16)
    hi, mid, lo = split3(rolled)
    return (dot(hi, onehot) + dot(mid, onehot) + dot(lo, onehot)) * LOG2E


def fold_table(acc):
    lane = lax.broadcasted_iota(jnp.int32, (PAIR, 256), 1)
    query = lax.broadcasted_iota(jnp.int32, (PAIR, 256), 0)
    onehot = (lane == 112 - lane_code(query)).astype(BF16)
    hi, mid, _ = split3(acc)
    wide = dot(hi, onehot) + dot(mid, onehot)
    total = jnp.zeros((WIN, 256), F32)
    for kr in range(WIN):
        total += pltpu.roll(
            wide[kr * WIN : (kr + 1) * WIN], 15 * kr, 1, stride=1, stride_axis=0
        )
    return jnp.sum(total, 0, keepdims=True)


def reverse_lanes(rows):
    a = lax.broadcasted_iota(jnp.int32, (256, 256), 0)
    b = lax.broadcasted_iota(jnp.int32, (256, 256), 1)
    onehot = (a + b == 224).astype(BF16)
    hi, mid, _ = split3(rows)
    return dot(hi, onehot) + dot(mid, onehot)


def norm(x):
    mean = jnp.sum(x, 0, keepdims=True) * (1.0 / C)
    centred = x - mean
    var = jnp.sum(centred * centred, 0, keepdims=True) * (1.0 / C)
    r = lax.rsqrt(var + 1e-05)
    return centred * r, r


def norm_back(dxhat, xhat, r):
    m1 = jnp.sum(dxhat, 0, keepdims=True) * (1.0 / C)
    m2 = jnp.sum(dxhat * xhat, 0, keepdims=True) * (1.0 / C)
    return r * (dxhat - m1 - xhat * m2)


def per_pair(v):
    return [v[:, p : p + PAIR] for p in range(0, v.shape[1], PAIR)]


def per_heads(v):
    step = HEADS * PAIR
    return [v[:, p : p + step] for p in range(0, v.shape[1], step)]


def across(ref, start, count):
    return jnp.concatenate([ref[start + p] for p in range(count)], 1)


def keep_pairs(ref, start, v):
    for p, part in enumerate(per_pair(v)):
        ref[start + p] = part


def scaled(v, gain):
    return jnp.concatenate([part * gain for part in per_pair(v)], 1)


def with_ones(v):
    return jnp.concatenate([v, jnp.ones((AUG - C, v.shape[1]), BF16)], 0)


def head_blocks(v):
    zero = jnp.zeros((HEAD, PAIR), v.dtype)
    cols = []
    for h in range(HEADS):
        rows = [v[g * HEAD : (g + 1) * HEAD] if g == h else zero for g in range(HEADS)]
        cols.append(jnp.concatenate(rows, 0))
    return jnp.concatenate(cols, 1)


def first_lanes(v):
    lane = lax.broadcasted_iota(jnp.int32, (1, v.shape[1]), 1)
    return (lane % PAIR) < 64


def window_rows(v):
    zero = jnp.zeros_like(v)
    first = jnp.broadcast_to(first_lanes(v), v.shape)
    return jnp.concatenate([jnp.where(first, v, zero), jnp.where(first, zero, v)], 0)


def deep_rows(v):
    pad = jnp.zeros((PAIR - C, HEADS * PAIR), v.dtype)
    return window_rows(jnp.concatenate([head_blocks(v), pad], 0))


def deep_tokens(v):
    pad = jnp.zeros((PAIR - C, PAIR), v.dtype)
    tokens = transposed(jnp.concatenate([v, pad], 0))
    return jnp.concatenate([tokens[:64], tokens[64:]], 1)


def head_diagonal(v):
    return jnp.concatenate(
        [v[h * HEAD : (h + 1) * HEAD, h * PAIR : (h + 1) * PAIR] for h in range(HEADS)], 0
    )


def gelu_parts(u):
    k = 0.7978845608028654
    uu = u * u
    half = 0.5 + 0.5 * jnp.tanh(u * (k + (k * 0.044715) * uu))
    m = u * half
    return m, half + m * (1.0 - half) * (2 * k + (6 * k * 0.044715) * uu)


def forward(x, b, w, penalty, keep=lambda n, v: None):
    xhat1, r1 = norm(x)
    keep(0, xhat1)
    keep(1, r1)
    a = with_ones(scaled(xhat1, w.gain[b, 0]).astype(BF16))
    keep(2, a)
    qkv = dot(w.qkv_t[b], a).astype(BF16)
    keep(3, qkv)
    parts = per_pair(qkv)
    scores = [dot(deep_tokens(part[C : 2 * C]), deep_rows(part[:C])) for part in parts]
    probs = []
    for p in range(0, len(parts), CHUNK):
        some = range(p, min(p + CHUNK, len(parts)))
        bias = jnp.concatenate([w.bias[b]] * len(some), 1)
        score = jnp.concatenate([scores[q] for q in some], 1) * (SCALE * LOG2E) + bias
        if penalty is not None:
            none = jnp.zeros((64, PAIR), F32)
            extra = [none if penalty[q] is None else penalty[q] for q in some]
            score = score + jnp.concatenate([v for v in extra for _ in range(HEADS)], 1)
        e = jnp.exp2(score - jnp.max(score, 0, keepdims=True))
        probs.append((e * (1.0 / jnp.sum(e, 0, keepdims=True))).astype(BF16))
    probs = jnp.concatenate(probs, 1)
    keep(4, probs)
    mixed = [
        head_diagonal(dot(part[2 * C :], window_rows(prob)))
        for part, prob in zip(parts, per_heads(probs))
    ]
    mix = jnp.concatenate(mixed, 1).astype(BF16)
    keep(5, mix)
    h = x + dot(w.proj_t[b], mix)
    xhat2, r2 = norm(h)
    keep(6, xhat2)
    keep(7, r2)
    f = with_ones(scaled(xhat2, w.gain[b, 1]).astype(BF16))
    keep(8, f)
    u = dot(w.up_t[b], f)
    m, slope = gelu_parts(u)
    m = m.astype(BF16)
    keep(9, m)
    keep(10, slope)
    out = h + dot(w.down_t[b], m)
    return out, (xhat1, r1, a, qkv, probs, mix, xhat2, r2, f, m, slope)


def backward(g, b, w, saved, mask):
    xhat1, r1, a, qkv, probs, mix, xhat2, r2, f, m, slope = saved

    def own(v):
        return v if mask is None else v * mask.astype(v.dtype)

    def pairs_sum(v):
        return sum(per_pair(v))

    g16 = g.astype(BF16)
    du = (dot(w.down[b], g16) * slope).astype(BF16)
    w.d_down[b] += dot_nt(own(g16), m)
    w.d_up[b] += dot_nt(own(f), du)
    df = dot(w.up[b], du)
    w.d_gain[b, 1] += pairs_sum(own(df * xhat2))
    dh = g + norm_back(scaled(df, w.gain[b, 1]), xhat2, r2)
    dh16 = dh.astype(BF16)
    w.d_proj[b] += dot_nt(mix, own(dh16))
    dmix = dot(w.proj[b], dh16).astype(BF16)
    parts, d_parts = per_pair(qkv), per_pair(dmix)
    dprobs = [dot(deep_tokens(v[2 * C :]), deep_rows(d)) for v, d in zip(parts, d_parts)]
    ds16 = []
    d_bias = jnp.zeros((64, HEADS * PAIR), F32)
    for p in range(0, len(parts), CHUNK):
        some = range(p, min(p + CHUNK, len(parts)))
        prob = probs[:, HEADS * PAIR * p : HEADS * PAIR * (p + len(some))].astype(F32)
        weighted = prob * jnp.concatenate([dprobs[q] for q in some], 1)
        ds = weighted - prob * jnp.sum(weighted, 0, keepdims=True)
        ds16.append(ds.astype(BF16))
        for q, part in zip(some, per_heads(ds)):
            if mask is not None:
                part = part * jnp.concatenate([per_pair(mask)[q]] * HEADS, 1)
            d_bias = d_bias + part
    w.d_bias[b] += d_bias
    dq, dk, dv = [], [], []
    ds16 = jnp.concatenate(ds16, 1)
    for part, d_part, prob, ds in zip(parts, d_parts, per_heads(probs), per_heads(ds16)):
        ds = window_rows(ds)
        dv.append(dot_nt(head_blocks(d_part), window_rows(prob)))
        dk.append(dot_nt(head_blocks(part[:C]), ds) * SCALE)
        dq.append(head_diagonal(dot(part[C : 2 * C], ds)) * SCALE)
    dqkv = jnp.concatenate([jnp.concatenate(v, 1) for v in (dq, dk, dv)], 0).astype(BF16)
    w.d_qkv[b] += dot_nt(own(a), dqkv)
    da = dot(w.qkv[b], dqkv)
    w.d_gain[b, 0] += pairs_sum(own(da * xhat1))
    return dh + norm_back(scaled(da, w.gain[b, 0]), xhat1, r1)


class Layers:
    pass


class PerLayer:
    def __init__(self, *refs):
        self.refs = refs

    def __getitem__(self, key):
        if isinstance(key, tuple):
            return self.refs[key[0]][key[1]]
        return self.refs[key][...]


def fetch(pairs, sems):
    copies = [pltpu.make_async_copy(src, dst, sems.at[n]) for n, (src, dst) in enumerate(pairs)]
    for copy in copies:
        copy.start()
    return copies


def finish(copies):
    for copy in copies:
        copy.wait()


def windows_t(ref, places, r0, c0):
    tokens = []
    for i, j in places:
        block = ref[r0 + WIN * i : r0 + WIN * (i + 1), c0 + WIN * j : c0 + WIN * (j + 1), :]
        tokens.append(block.astype(F32).reshape(WIN * WIN, C))
    if len(tokens) == 1:
        tokens.append(jnp.zeros((WIN * WIN, C), F32))
    return jnp.transpose(jnp.concatenate(tokens, 0))


def windows_back(value, ref, places):
    tokens = jnp.transpose(value)
    for n, (i, j) in enumerate(places):
        block = tokens[n * 64 : (n + 1) * 64].reshape(WIN, WIN, C)
        ref[WIN * i : WIN * (i + 1), WIN * j : WIN * (j + 1), :] = block.astype(ref.dtype)


VMEM = pl.BlockSpec(memory_space=pltpu.VMEM)
HBM = pl.BlockSpec(memory_space=pltpu.HBM)
COL_AXES = ("col_half", "core")
SAVES = [
    ((OWN_PAIRS, C, PAIR), F32),
    ((OWN_PAIRS, 1, PAIR), F32),
    ((OWN_PAIRS, AUG, PAIR), BF16),
    ((OWN_PAIRS, 3 * C, PAIR), BF16),
    ((OWN_PAIRS, 64, HEADS * PAIR), BF16),
    ((OWN_PAIRS, C, PAIR), BF16),
    ((OWN_PAIRS, C, PAIR), F32),
    ((OWN_PAIRS, 1, PAIR), F32),
    ((OWN_PAIRS, AUG, PAIR), BF16),
    ((OWN_PAIRS, HID, PAIR), BF16),
    ((OWN_PAIRS, HID, PAIR), BF16),
]


def shapes(entries):
    return [jax.ShapeDtypeStruct(shape, kind) for shape, kind in entries]


def scratch(entries):
    return [pltpu.VMEM(shape, kind) for shape, kind in entries]


def sides(position, from_a, from_b):
    even = position % 2 == 0
    return jnp.where(even, from_b, from_a), jnp.where(even, from_a, from_b)


def to_sides(position, before, after):
    even = position % 2 == 0
    return jnp.where(even, after, before), jnp.where(even, before, after)


def wide_gains(norm_gains, b):
    rows = [jnp.broadcast_to(norm_gains[b, n : n + 1, :], (PAIR, C)) for n in range(2)]
    return [jnp.transpose(row) for row in rows]


def keep_bias(bias, table, bias_table, b):
    table[...] = jnp.zeros(table.shape, F32)
    for h in range(HEADS):
        table[h : h + 1, 0 : bias_table.shape[2]] = bias_table[h, b : b + 1, :]
        bias[:, h * PAIR : (h + 1) * PAIR] = expand_table(table[h : h + 1, :])


GAIN = ((2, C, PAIR), F32)
BIAS = ((64, HEADS * PAIR), F32)
QKV_T = ((3 * C, AUG), BF16)
PROJ_T = ((C, C), BF16)
UP_T = ((HID, AUG), BF16)
DOWN = ((HID, C), BF16)
TABLE = ((8, 256), F32)
SMALL = [((2, 2, C), F32), ((2, 3 * C), F32), ((HEADS, 2, 225), F32), ((2, HID), F32)]
WEIGHTS = [((2, C, 3 * C), BF16), ((2, C, C), BF16), ((2, C, HID), BF16), ((2, C, HID), BF16)]
FIRST = [((C, 3 * C), BF16), ((C, C), BF16), ((C, HID), BF16), ((C, HID), BF16)]
TILE = ((TH, TW, C), BF16)


def lower_kernel(
    region,
    cot,
    norm_gains,
    qkv_bias,
    bias_table,
    up_bias,
    qkv_weight,
    proj_weight,
    up_weight,
    down_t,
    low_far,
    far_a,
    far_b,
    *rest,
):
    saves, rest = rest[: len(SAVES)], rest[len(SAVES) :]
    sems, field, table, gain, bias, tile, cot_tile, low, send_a, send_b, *rest = rest
    small, weights, kept = rest[:4], rest[4:8], rest[8:]
    sources = [norm_gains, qkv_bias, bias_table, up_bias]
    sources += [ref.at[0] for ref in (qkv_weight, proj_weight, up_weight, down_t)]
    copies = fetch(zip(sources + [region, cot], small + weights + [tile, cot_tile]), sems)
    w = Layers()
    finish(copies[:8])
    norm_gains, qkv_bias, bias_table, up_bias = small
    gain[0], gain[1] = wide_gains(norm_gains, 0)
    keep_bias(bias, table, bias_table, 0)
    w.gain, w.bias, w.down_t = PerLayer(gain), PerLayer(bias), PerLayer(weights[3])
    w.qkv_t = [augmented(weights[0][...], qkv_bias[0:1, :])]
    w.proj_t = [transposed(weights[1][...])]
    w.up_t = [augmented(weights[2][...], up_bias[0:1, :])]
    finish(copies[8:])
    x = [windows_t(tile, LOWER[2 * n : 2 * n + 2], 0, 0) for n in range(OWN_PAIRS)]
    leaving = []

    def keep(k, value):
        ref = kept[k]
        parts = per_heads(value) if ref.shape[2] == HEADS * PAIR else per_pair(value)
        for n, part in enumerate(parts):
            ref[n] = part.astype(ref.dtype)
        leaving.append(pltpu.make_async_copy(ref, saves[k], sems.at[13 + k]))
        leaving[-1].start()

    y, _ = forward(jnp.concatenate(x, 1), 0, w, None, keep)
    for n, part in enumerate(per_pair(y)):
        windows_back(part, field, LOWER[2 * n : 2 * n + 2])
    value = field[...].astype(BF16)
    low[...] = value
    top = jnp.concatenate([value[0:4], cot_tile[0:4]], 0)
    bottom = jnp.concatenate([value[TH - 4 :], cot_tile[TH - 4 :]], 0)
    near_part, far_part = to_sides(lax.axis_index("row"), top, bottom)
    send_a[...] = near_part
    send_b[...] = far_part
    leaving += fetch([(low, low_far), (send_a, far_a), (send_b, far_b)], sems.at[pl.ds(10, 3)])
    finish(leaving)


def prepare_kernel(
    after,
    norm_gains,
    qkv_bias,
    bias_table,
    up_bias,
    qkv_weight,
    proj_weight,
    up_weight,
    down_t,
    *rest,
):
    far, (sems, table), rest = rest[:8], rest[8:10], rest[10:]
    (qkv, proj, up, down_copy), small, made = rest[:4], rest[4:8], rest[8:]
    gain_0, gain_1, bias, qkv_t, proj_t, up_t, down_0, down_1 = made
    sources = [norm_gains, qkv_bias, bias_table, up_bias]
    sources += [qkv_weight, proj_weight, up_weight, down_t]
    finish(fetch(zip(sources, list(small) + [qkv, proj, up, down_copy]), sems))
    norm_gains, qkv_bias, bias_table, up_bias = small
    for b, gain in enumerate((gain_0, gain_1)):
        gain[0], gain[1] = wide_gains(norm_gains, b)
    keep_bias(bias, table, bias_table, 1)
    qkv_t[...] = augmented(qkv[1], qkv_bias[1:2, :])
    proj_t[...] = transposed(proj[1])
    up_t[...] = augmented(up[1], up_bias[1:2, :])
    down_0[...] = transposed(down_copy[0])
    down_1[...] = transposed(down_copy[1])
    finish(fetch(zip(made, far), sems))


PREPARED = [GAIN, GAIN, BIAS, QKV_T, PROJ_T, UP_T, DOWN, DOWN]


def strip_kernel(*refs):
    sources, (far_a, far_b, sems, send_a, send_b), places = refs[:4], refs[4:9], refs[9:]
    finish(fetch(zip(sources, places), sems))
    row = lax.axis_index("row")
    both = []
    for cols in (slice(0, 8), slice(TW - 8, TW)):
        strips = []
        for n, own in enumerate(places[:2]):
            above, below = sides(row, places[2][4 * n : 4 * n + 4], places[3][4 * n : 4 * n + 4])
            tall = [v.astype(F32) for v in (above[:, cols], own[:, cols], below[:, cols])]
            tall = jnp.concatenate(tall, 0)
            half = tall[:, 0:4] if cols.start == 0 else tall[:, 4:8]
            strips.append(jnp.concatenate([half[0:12], half[12:24]], 1))
        both.append(jnp.concatenate(strips, 0).astype(BF16))
    near_part, far_part = to_sides(lax.axis_index(COL_AXES), *both)
    send_a[...] = near_part
    send_b[...] = far_part
    finish(fetch([(send_a, far_a), (send_b, far_b)], sems))


UPPER_IN = [TILE, TILE] + [((8, TW, C), BF16)] * 2 + [((24, 8, C), BF16)] * 2
UPPER_IN += WEIGHTS + PREPARED + SAVES


def upper_kernel(rows_cols, *rest):
    sources, rest = rest[: len(UPPER_IN)], rest[len(UPPER_IN) :]
    out_far, grad_far, keep_far, give_far, sems, out, grad_region, packed, *rest = rest
    local_in, rest = rest[: len(UPPER_IN)], rest[len(UPPER_IN) :]
    low_field, cot_field, out_field, grad_field, table, misc, *rest = rest
    d_gain, d_qkv, d_proj, d_up, d_down, d_bias = rest
    copies = fetch(zip(sources, local_in), sems)
    low, cot_tile = local_in[:2]
    got_row, got_col = local_in[2:4], local_in[4:6]
    prepared, saves = local_in[10:18], local_in[18:]

    w = Layers()
    w.qkv, w.proj, w.up, w.down_t = local_in[6:10]
    w.gain = PerLayer(*prepared[:2])
    w.bias, w.qkv_t, w.proj_t, w.up_t = [PerLayer(None, ref) for ref in prepared[2:6]]
    w.down = PerLayer(*prepared[6:])
    w.d_gain, w.d_qkv, w.d_proj = d_gain, d_qkv, d_proj
    w.d_up, w.d_down, w.d_bias = d_up, d_down, d_bias
    row, col = lax.axis_index("row"), lax.axis_index(COL_AXES)
    first_row, last_row = row == 0, row == rows_cols[0] - 1
    first_col, last_col = col == 0, col == rows_cols[1] - 1

    for ref in (d_gain, d_qkv, d_proj, d_up, d_down, d_bias, misc):
        ref[...] = jnp.zeros(ref.shape, F32)
    table[...] = jnp.zeros(table.shape, F32)
    finish(copies[:6])
    left, right = sides(col, got_col[0][...].astype(F32), got_col[1][...].astype(F32))
    inner = slice(8, 8 + TW)
    for n, (field, own) in enumerate(((low_field, low), (cot_field, cot_tile))):
        part = slice(4 * n, 4 * n + 4)
        above, below = sides(row, got_row[0][part], got_row[1][part])
        field[0:4, inner, :] = above.astype(F32)
        field[4 : 4 + TH, inner, :] = own[...].astype(F32)
        field[4 + TH :, inner, :] = below.astype(F32)
        for half in range(2):
            rows = slice(12 * half, 12 * half + 12)
            from_rows, from_cols = slice(12 * n, 12 * n + 12), slice(4 * half, 4 * half + 4)
            field[rows, 4:8, :] = left[from_rows, from_cols, :]
            field[rows, 8 + TW : 12 + TW, :] = right[from_rows, from_cols, :]

    def edges(s):
        i, j = UPPER[s] if s < len(UPPER) else (1, 1)
        flags = (first_row, i == 0), (last_row, i == 2), (first_col, j == 0), (last_col, j == 6)
        return [jnp.where(flag, FAR, 0.0) if here else 0.0 for flag, here in flags]

    places = [UPPER[2 * n : 2 * n + 2] for n in range(UPPER_PAIRS)]
    key = lax.broadcasted_iota(jnp.int32, (64, PAIR), 0)
    first = lax.broadcasted_iota(jnp.int32, (64, PAIR), 1) < 64
    upper_half = (key // WIN) < 4
    left_half = (key % WIN) < 4
    penalty = []
    for n in range(UPPER_PAIRS):
        one, two = edges(2 * n), edges(2 * n + 1)
        if all(i == 1 and 0 < j < 6 for i, j in places[n]):
            penalty.append(None)
            continue
        top, bottom, before, after = [jnp.where(first, v, u) for v, u in zip(one, two)]
        penalty.append(jnp.where(upper_half, top, bottom) + jnp.where(left_half, before, after))
    slot = lax.broadcasted_iota(jnp.int32, (1, UPPER_PAIRS * PAIR), 1) // 64
    row_own = jnp.where(last_row, 1.0, 0.0)
    col_own = jnp.where(last_col, 1.0, 0.0)
    mask = jnp.where(
        slot < 12,
        1.0,
        jnp.where(
            slot < 18,
            row_own,
            jnp.where(slot < 19, row_own * col_own, jnp.where(slot < 21, col_own, 0.0)),
        ),
    )

    finish(copies[6:18])
    x = jnp.concatenate([windows_t(low_field, p, 0, 4) for p in places], 1)
    g = jnp.concatenate([windows_t(cot_field, p, 0, 4) for p in places], 1)
    y, saved = forward(x, 1, w, penalty)
    for p, part in zip(places, per_pair(y)):
        windows_back(part, out_field, p)
    out[...] = out_field[4 : 4 + TH, 4 : 4 + TW, :].astype(BF16)
    leaving = fetch([(out, out_far)], sems)
    dx = backward(g, 1, w, saved, mask)
    for p, part in zip(places, per_pair(dx)):
        windows_back(part, grad_field, p)

    g = jnp.concatenate([windows_t(grad_field, p, 4, 4) for p in places[:OWN_PAIRS]], 1)
    finish(copies[18:])
    saved = [jnp.concatenate([ref[n] for n in range(OWN_PAIRS)], 1) for ref in saves]
    dx = backward(g, 0, w, saved, None)
    for p, part in zip(places, per_pair(dx)):
        windows_back(part, grad_region, p)
    leaving += fetch([(grad_region, grad_far)], sems.at[pl.ds(1, 1)])

    for b in range(2):
        for j in range(3):
            lanes = slice(j * PAIR, (j + 1) * PAIR)
            packed[b, j * C : (j + 1) * C, :] = d_up[b, 0:C, lanes].astype(BF16)
            packed[b, 288 + j * C : 288 + (j + 1) * C, :] = d_down[b, :, lanes].astype(BF16)
            misc[b, 3 + j : 4 + j, :] = d_up[b, C : C + 1, lanes]
        for j in range(2):
            lanes = slice(j * PAIR, (j + 1) * PAIR)
            packed[b, 576 + j * C : 576 + (j + 1) * C, :] = d_qkv[b, 0:C, lanes].astype(BF16)
            misc[b, j : j + 1, :] = d_qkv[b, C : C + 1, lanes]
        last = jnp.concatenate([d_qkv[b, 0:C, 256:288], d_proj[b]], 1)
        packed[b, 768:864, :] = last.astype(BF16)
        misc[b, 2:3, 0:32] = d_qkv[b, C : C + 1, 256:288]
        for n in range(2):
            column = jnp.sum(jnp.transpose(d_gain[b, n]), 0, keepdims=True)
            misc[b, 6 + n : 7 + n, 0:C] = column
        for h in range(HEADS):
            table[h : h + 1, :] = fold_table(d_bias[b, :, h * PAIR : (h + 1) * PAIR])
        rows = reverse_lanes(table[...])
        misc[b, 8:16, :] = rows[:, 0:PAIR]
        misc[b, 16:24, :] = rows[:, PAIR:]
        packed[b, 864:896, :] = misc[b].astype(BF16)
        packed[b, 896:ROWS, :] = jnp.zeros((ROWS - 896, PAIR), BF16)
    core = lax.axis_index("core")
    pairs = [(packed.at[core], keep_far), (packed.at[1 - core], give_far)]
    finish(leaving + fetch(pairs, sems.at[pl.ds(2, 2)]))


def unpack_kernel(
    mine_far, other_far, gains, qkv, qkv_bias, table, proj, up, up_bias, down_t, sems, mine, other
):
    finish(fetch([(mine_far, mine), (other_far, other)], sems))
    core = lax.axis_index("core")
    for b in range(2):
        flat = jnp.where(core == b, mine[...], other[...]).astype(F32)
        misc = flat[864:896]
        for j in range(3):
            lanes = slice(j * PAIR, (j + 1) * PAIR)
            up[b, :, lanes] = flat[j * C : (j + 1) * C]
            down_t[b, :, lanes] = flat[288 + j * C : 288 + (j + 1) * C]
            up_bias[b : b + 1, lanes] = misc[3 + j : 4 + j]
        for j in range(2):
            lanes = slice(j * PAIR, (j + 1) * PAIR)
            qkv[b, :, lanes] = flat[576 + j * C : 576 + (j + 1) * C]
            qkv_bias[b : b + 1, lanes] = misc[j : j + 1]
        last = flat[768:864]
        qkv[b, :, 256:288] = last[:, 0:32]
        proj[b] = last[:, 32:PAIR]
        qkv_bias[b : b + 1, 256:288] = misc[2:3, 0:32]
        for n in range(2):
            gains[b, n : n + 1, :] = misc[6 + n : 7 + n, 0:C]
        for h in range(HEADS):
            table[h, b : b + 1, 0:PAIR] = misc[8 + h : 9 + h]
            table[h, b : b + 1, PAIR:225] = misc[16 + h : 17 + h, 0:97]


def near(count):
    return [(i, i ^ 1) for i in range(count)]


def far(count):
    return [(i, ((i - 1) ^ 1) + 1) for i in range(1, count - 1)]


def swap(pair, axes, count):
    return lax.ppermute(pair[0], axes, near(count)), lax.ppermute(pair[1], axes, far(count))


def body(region, cotangent, gains, qkv, qkv_bias, table, proj, up, up_bias, down):
    rows, cols = lax.axis_size("row"), lax.axis_size(COL_AXES)
    table_t = jnp.transpose(table, (1, 0, 2))
    down_t = jnp.transpose(down, (0, 2, 1))
    params = (gains, qkv_bias, table_t, up_bias, qkv, proj, up, down_t)
    limit = pltpu.CompilerParams(vmem_limit_bytes=LIMIT)

    def dma(count):
        return [pltpu.SemaphoreType.DMA((count,))]

    strip = ((8, TW, C), BF16)
    low, send_a, send_b, *saved = pl.pallas_call(
        lower_kernel,
        out_shape=shapes([TILE, strip, strip] + SAVES),
        in_specs=[HBM] * 10,
        out_specs=[HBM] * (3 + len(SAVES)),
        scratch_shapes=dma(13 + len(SAVES))
        + scratch([((TH, TW, C), F32), TABLE, GAIN, BIAS, TILE, TILE, TILE, strip, strip])
        + scratch(SMALL + FIRST + SAVES),
        compiler_params=limit,
        name="lower",
    )(region, cotangent, *params)
    row_got = swap((send_a, send_b), "row", rows)
    prepared = pl.pallas_call(
        prepare_kernel,
        out_shape=shapes(PREPARED),
        in_specs=[HBM] * 9,
        out_specs=[HBM] * len(PREPARED),
        scratch_shapes=dma(8) + scratch([TABLE] + WEIGHTS + SMALL + PREPARED),
        compiler_params=limit,
        cost_estimate=pl.CostEstimate(flops=10**9, bytes_accessed=4 * 10**6, transcendentals=0),
        name="prepare",
    )(saved[1], *params)
    strip = ((24, 8, C), BF16)
    send = pl.pallas_call(
        strip_kernel,
        out_shape=shapes([strip, strip]),
        in_specs=[HBM] * 4,
        out_specs=[HBM] * 2,
        scratch_shapes=dma(4) + scratch([strip, strip] + UPPER_IN[:4]),
        compiler_params=limit,
        name="strips",
    )(low, cotangent, *row_got)
    col_got = swap(send, COL_AXES, cols)
    wide = ((TH + 8, TW + 16, C), F32)
    narrow = ((TH + 8, TW + 8, C), F32)
    sums = [
        ((2, 2, C, PAIR), F32),
        ((2, AUG, 3 * C), F32),
        ((2, C, C), F32),
        ((2, AUG, HID), F32),
        ((2, C, HID), F32),
        ((2, 64, HEADS * PAIR), F32),
    ]
    results = [TILE, ((TH, TW, C), F32)]
    flat = ((ROWS, PAIR), BF16)
    out, grad_region, keep, give = pl.pallas_call(
        functools.partial(upper_kernel, (rows, cols)),
        out_shape=shapes(results + [flat, flat]),
        in_specs=[HBM] * len(UPPER_IN),
        out_specs=[HBM] * 4,
        scratch_shapes=dma(len(UPPER_IN))
        + scratch(results + [((2, ROWS, PAIR), BF16)] + UPPER_IN + [wide, wide, narrow, narrow, TABLE, ((2, 32, PAIR), F32)] + sums),
        compiler_params=limit,
        name="upper",
    )(low, cotangent, *row_got, *col_got, qkv, proj, up, down_t, *prepared, *saved)
    got = lax.ppermute(give, "core", near(2))
    share = (keep.astype(F32) + got.astype(F32)).astype(BF16).reshape(PEERS, -1, PAIR)
    peers = ("row", "col_half")
    parts = lax.all_to_all(share, peers, 0, 0)
    part = jnp.sum(parts.astype(F32), 0, keepdims=True).astype(BF16)
    mine = lax.all_to_all(jnp.broadcast_to(part, share.shape), peers, 0, 0)
    mine = mine.reshape(ROWS, PAIR)
    other = lax.ppermute(mine, "core", near(2))
    grads = pl.pallas_call(
        unpack_kernel,
        out_shape=tuple(
            jax.ShapeDtypeStruct(shape, F32)
            for shape in (
                (2, 2, C),
                (2, C, 3 * C),
                (2, 3 * C),
                (HEADS, 2, 225),
                (2, C, C),
                (2, C, HID),
                (2, HID),
                (2, C, HID),
            )
        ),
        in_specs=[HBM] * 2,
        out_specs=[VMEM] * 8,
        scratch_shapes=dma(2) + scratch([flat, flat]),
        compiler_params=limit,
        name="unpack",
    )(mine, other)
    d_gains, d_qkv, d_qkv_bias, d_table, d_proj, d_up, d_up_bias, d_down_t = grads
    return (
        out,
        grad_region,
        d_gains,
        d_qkv,
        d_qkv_bias,
        jnp.transpose(d_table, (1, 0, 2)),
        d_proj,
        d_up,
        d_up_bias,
        jnp.transpose(d_down_t, (0, 2, 1)),
    )


def solution(mesh):
    rows, cols = mesh.devices.shape
    fine = Mesh(mesh.devices.reshape(rows, cols // 2, 2), ("row", "col_half", "core"))
    tile = P("row", ("col_half", "core"), None)
    return jax.shard_map(
        body,
        mesh=fine,
        in_specs=(tile, tile) + (P(),) * 8,
        out_specs=(tile, tile) + (P(),) * 8,
        check_vma=False,
    )
```

```python
import functools

import jax
import jax.numpy as jnp
from jax import lax
from jax.experimental import pallas as pl
from jax.experimental.pallas import tpu as pltpu
from jax.sharding import Mesh
from jax.sharding import PartitionSpec as P

C = 96
HEADS = 3
HEAD = 32
HID = 384
WIN = 8
TH = 16
TW = 48
AUG = 112
PAIR = 128
ROWS = 1024
PEERS = 128
LOG2E = 1.4426950408889634
SCALE = HEAD**-0.5
FAR = -1e30
F32 = jnp.float32
BF16 = jnp.bfloat16

LOWER = [(i, j) for i in (0, 1) for j in range(6)]
UPPER = LOWER + [(2, j) for j in range(7)] + [(0, 6), (1, 6)]
OWN_PAIRS = 6
UPPER_PAIRS = 11
CHUNK = 2
FEED = 256


def dot(a, b):
    return jnp.dot(a, b, preferred_element_type=F32)


def dot_nt(a, b):
    return lax.dot_general(a, b, (((1,), (1,)), ((), ())), preferred_element_type=F32)


def split3(v):
    hi = v.astype(BF16)
    rest = v - hi.astype(F32)
    mid = rest.astype(BF16)
    return hi, mid, (rest - mid.astype(F32)).astype(BF16)


def transposed(v):
    return jnp.transpose(v.astype(F32)).astype(BF16)


def augmented(weight, bias):
    hi, mid, lo = split3(bias)
    rows = lax.broadcasted_iota(jnp.int32, (AUG - C, bias.shape[1]), 0)
    extra = jnp.where(
        rows == 0,
        hi.astype(F32),
        jnp.where(rows == 1, mid.astype(F32), jnp.where(rows == 2, lo.astype(F32), 0.0)),
    )
    return transposed(jnp.concatenate([weight.astype(F32), extra], 0))


def lane_code(lanes):
    token = lanes % 64
    return (token // WIN) * 15 + token % WIN


def expand_table(row):
    parts = []
    for kr in range(WIN):
        wide = jnp.broadcast_to(row, (WIN, 256))
        parts.append(pltpu.roll(wide, (15 * kr - 112) % 256, 1, stride=1, stride_axis=0))
    rolled = jnp.concatenate(parts, 0)
    lane = lax.broadcasted_iota(jnp.int32, (256, PAIR), 0)
    query = lax.broadcasted_iota(jnp.int32, (256, PAIR), 1)
    onehot = (lane == lane_code(query)).astype(BF16)
    hi, mid, lo = split3(rolled)
    return (dot(hi, onehot) + dot(mid, onehot) + dot(lo, onehot)) * LOG2E


def fold_table(acc):
    lane = lax.broadcasted_iota(jnp.int32, (PAIR, 256), 1)
    query = lax.broadcasted_iota(jnp.int32, (PAIR, 256), 0)
    onehot = (lane == 112 - lane_code(query)).astype(BF16)
    hi, mid, _ = split3(acc)
    wide = dot(hi, onehot) + dot(mid, onehot)
    total = jnp.zeros((WIN, 256), F32)
    for kr in range(WIN):
        total += pltpu.roll(
            wide[kr * WIN : (kr + 1) * WIN], 15 * kr, 1, stride=1, stride_axis=0
        )
    return jnp.sum(total, 0, keepdims=True)


def reverse_lanes(rows):
    a = lax.broadcasted_iota(jnp.int32, (256, 256), 0)
    b = lax.broadcasted_iota(jnp.int32, (256, 256), 1)
    onehot = (a + b == 224).astype(BF16)
    hi, mid, _ = split3(rows)
    return dot(hi, onehot) + dot(mid, onehot)


def norm(x):
    mean = jnp.sum(x, 0, keepdims=True) * (1.0 / C)
    centred = x - mean
    var = jnp.sum(centred * centred, 0, keepdims=True) * (1.0 / C)
    r = lax.rsqrt(var + 1e-05)
    return centred * r, r


def norm_back(dxhat, xhat, r):
    m1 = jnp.sum(dxhat, 0, keepdims=True) * (1.0 / C)
    m2 = jnp.sum(dxhat * xhat, 0, keepdims=True) * (1.0 / C)
    return r * (dxhat - m1 - xhat * m2)


def per_pair(v):
    return [v[:, p : p + PAIR] for p in range(0, v.shape[1], PAIR)]


def per_heads(v):
    step = HEADS * PAIR
    return [v[:, p : p + step] for p in range(0, v.shape[1], step)]


def split_lanes(v):
    return [v[:, p : p + FEED] for p in range(0, v.shape[1], FEED)]


def scaled(v, gain):
    return jnp.concatenate([part * gain for part in per_pair(v)], 1)


def with_ones(v):
    return jnp.concatenate([v, jnp.ones((AUG - C, v.shape[1]), BF16)], 0)


def head_blocks(v):
    zero = jnp.zeros((HEAD, PAIR), v.dtype)
    cols = []
    for h in range(HEADS):
        rows = [v[g * HEAD : (g + 1) * HEAD] if g == h else zero for g in range(HEADS)]
        cols.append(jnp.concatenate(rows, 0))
    return jnp.concatenate(cols, 1)


def first_lanes(v):
    lane = lax.broadcasted_iota(jnp.int32, (1, v.shape[1]), 1)
    return (lane % PAIR) < 64


def window_rows(v):
    zero = jnp.zeros_like(v)
    first = jnp.broadcast_to(first_lanes(v), v.shape)
    return jnp.concatenate([jnp.where(first, v, zero), jnp.where(first, zero, v)], 0)


def deep_rows(v):
    pad = jnp.zeros((PAIR - C, HEADS * PAIR), v.dtype)
    return window_rows(jnp.concatenate([head_blocks(v), pad], 0))


def deep_tokens(v):
    pad = jnp.zeros((PAIR - C, PAIR), v.dtype)
    tokens = transposed(jnp.concatenate([v, pad], 0))
    return jnp.concatenate([tokens[:64], tokens[64:]], 1)


def by_head(rows, blocks, product):
    return jnp.concatenate(
        [
            product(rows[h * HEAD : (h + 1) * HEAD], blocks[:, h * PAIR : (h + 1) * PAIR])
            for h in range(HEADS)
        ],
        0,
    )


def gelu_parts(u):
    k = 0.7978845608028654
    uu = u * u
    half = 0.5 + 0.5 * jnp.tanh(u * (k + (k * 0.044715) * uu))
    m = u * half
    return m, half + m * (1.0 - half) * (2 * k + (6 * k * 0.044715) * uu)


def forward(x, b, w, penalty, keep=lambda n, v: None):
    xhat1, r1 = norm(x)
    keep(0, xhat1)
    keep(1, r1)
    a = with_ones(scaled(xhat1, w.gain[b, 0]).astype(BF16))
    keep(2, a)
    qkv = dot(w.qkv_t[b], a).astype(BF16)
    keep(3, qkv)
    parts = per_pair(qkv)
    scores = [dot(deep_tokens(part[C : 2 * C]), deep_rows(part[:C])) for part in parts]
    probs = []
    for p in range(0, len(parts), CHUNK):
        some = range(p, min(p + CHUNK, len(parts)))
        bias = jnp.concatenate([w.bias[b]] * len(some), 1)
        score = jnp.concatenate([scores[q] for q in some], 1) * (SCALE * LOG2E) + bias
        if penalty is not None:
            none = jnp.zeros((64, PAIR), F32)
            extra = [none if penalty[q] is None else penalty[q] for q in some]
            score = score + jnp.concatenate([v for v in extra for _ in range(HEADS)], 1)
        e = jnp.exp2(score - jnp.max(score, 0, keepdims=True))
        probs.append((e * (1.0 / jnp.sum(e, 0, keepdims=True))).astype(BF16))
    probs = jnp.concatenate(probs, 1)
    keep(4, probs)
    mixed = [
        by_head(part[2 * C :], window_rows(prob), dot)
        for part, prob in zip(parts, per_heads(probs))
    ]
    mix = jnp.concatenate(mixed, 1).astype(BF16)
    keep(5, mix)
    h = x + dot(w.proj_t[b], mix)
    xhat2, r2 = norm(h)
    keep(6, xhat2)
    keep(7, r2)
    f = with_ones(scaled(xhat2, w.gain[b, 1]).astype(BF16))
    keep(8, f)
    m, slope = [], []
    for part in split_lanes(f):
        one, two = gelu_parts(dot(w.up_t[b], part))
        m.append(one.astype(BF16))
        slope.append(two.astype(BF16))
    m, slope = jnp.concatenate(m, 1), jnp.concatenate(slope, 1)
    keep(9, m)
    keep(10, slope)
    out = h + dot(w.down_t[b], m)
    return out, (xhat1, r1, a, qkv, probs, mix, xhat2, r2, f, m, slope)


def backward(g, b, w, saved, mask):
    xhat1, r1, a, qkv, probs, mix, xhat2, r2, f, m, slope = saved

    def own(v):
        return v if mask is None else v * mask.astype(v.dtype)

    def pairs_sum(v):
        return sum(per_pair(v))

    g16 = g.astype(BF16)
    du = []
    for part, part_slope in zip(split_lanes(g16), split_lanes(slope)):
        du.append((dot(w.down[b], part) * part_slope.astype(F32)).astype(BF16))
    du = jnp.concatenate(du, 1)
    w.d_down[b] = dot_nt(own(g16), m)
    w.d_up[b] = dot_nt(own(f), du)
    df = dot(w.up[b], du)
    w.d_gain[b, 1] = pairs_sum(own(df * xhat2))
    dh = g + norm_back(scaled(df, w.gain[b, 1]), xhat2, r2)
    dh16 = dh.astype(BF16)
    w.d_proj[b] = dot_nt(mix, own(dh16))
    dmix = dot(w.proj[b], dh16).astype(BF16)
    parts, d_parts = per_pair(qkv), per_pair(dmix)
    dprobs = [dot(deep_tokens(v[2 * C :]), deep_rows(d)) for v, d in zip(parts, d_parts)]
    ds16 = []
    d_bias = None
    for p in range(0, len(parts), CHUNK):
        some = range(p, min(p + CHUNK, len(parts)))
        prob = probs[:, HEADS * PAIR * p : HEADS * PAIR * (p + len(some))].astype(F32)
        weighted = prob * jnp.concatenate([dprobs[q] for q in some], 1)
        ds = weighted - prob * jnp.sum(weighted, 0, keepdims=True)
        ds16.append(ds.astype(BF16))
        for q, part in zip(some, per_heads(ds)):
            if mask is not None:
                part = part * jnp.concatenate([per_pair(mask)[q]] * HEADS, 1)
            d_bias = part if d_bias is None else d_bias + part
    w.d_bias[b] = d_bias
    dq, dk, dv = [], [], []
    ds16 = jnp.concatenate(ds16, 1)
    for part, d_part, prob, ds in zip(parts, d_parts, per_heads(probs), per_heads(ds16)):
        ds = window_rows(ds)
        dv.append(by_head(d_part, window_rows(prob), dot_nt))
        dk.append(by_head(part[:C], ds, dot_nt) * SCALE)
        dq.append(by_head(part[C : 2 * C], ds, dot) * SCALE)
    dqkv = jnp.concatenate([jnp.concatenate(v, 1) for v in (dq, dk, dv)], 0).astype(BF16)
    w.d_qkv[b] = dot_nt(own(a), dqkv)
    da = dot(w.qkv[b], dqkv)
    w.d_gain[b, 0] = pairs_sum(own(da * xhat1))
    return dh + norm_back(scaled(da, w.gain[b, 0]), xhat1, r1)


class Layers:
    pass


class PerLayer:
    def __init__(self, *refs):
        self.refs = refs

    def __getitem__(self, key):
        if isinstance(key, tuple):
            return self.refs[key[0]][key[1]]
        return self.refs[key][...]


def fetch(pairs, sems):
    copies = [pltpu.make_async_copy(src, dst, sems.at[n]) for n, (src, dst) in enumerate(pairs)]
    for copy in copies:
        copy.start()
    return copies


def finish(copies):
    for copy in copies:
        copy.wait()


def windows_t(ref, places, r0, c0):
    tokens = []
    for i, j in places:
        block = ref[r0 + WIN * i : r0 + WIN * (i + 1), c0 + WIN * j : c0 + WIN * (j + 1), :]
        tokens.append(block.astype(F32).reshape(WIN * WIN, C))
    if len(tokens) == 1:
        tokens.append(jnp.zeros((WIN * WIN, C), F32))
    return jnp.transpose(jnp.concatenate(tokens, 0))


def windows_back(value, ref, places):
    tokens = jnp.transpose(value)
    for n, (i, j) in enumerate(places):
        block = tokens[n * 64 : (n + 1) * 64].reshape(WIN, WIN, C)
        ref[WIN * i : WIN * (i + 1), WIN * j : WIN * (j + 1), :] = block.astype(ref.dtype)


VMEM = pl.BlockSpec(memory_space=pltpu.VMEM)
HBM = pl.BlockSpec(memory_space=pltpu.HBM)
COL_AXES = ("col_half", "core")
SAVES = [
    ((OWN_PAIRS, C, PAIR), F32),
    ((OWN_PAIRS, 1, PAIR), F32),
    ((OWN_PAIRS, AUG, PAIR), BF16),
    ((OWN_PAIRS, 3 * C, PAIR), BF16),
    ((OWN_PAIRS, 64, HEADS * PAIR), BF16),
    ((OWN_PAIRS, C, PAIR), BF16),
    ((OWN_PAIRS, C, PAIR), F32),
    ((OWN_PAIRS, 1, PAIR), F32),
    ((OWN_PAIRS, AUG, PAIR), BF16),
    ((OWN_PAIRS, HID, PAIR), BF16),
    ((OWN_PAIRS, HID, PAIR), BF16),
]


def shapes(entries):
    return [jax.ShapeDtypeStruct(shape, kind) for shape, kind in entries]


def scratch(entries):
    return [pltpu.VMEM(shape, kind) for shape, kind in entries]


def sides(position, from_a, from_b):
    even = position % 2 == 0
    return jnp.where(even, from_b, from_a), jnp.where(even, from_a, from_b)


def to_sides(position, before, after):
    even = position % 2 == 0
    return jnp.where(even, after, before), jnp.where(even, before, after)


def wide_gains(norm_gains, b):
    rows = [jnp.broadcast_to(norm_gains[b, n : n + 1, :], (PAIR, C)) for n in range(2)]
    return [jnp.transpose(row) for row in rows]


def keep_bias(bias, table, bias_table, b):
    table[...] = jnp.zeros(table.shape, F32)
    for h in range(HEADS):
        table[h : h + 1, 0 : bias_table.shape[2]] = bias_table[h, b : b + 1, :]
        bias[:, h * PAIR : (h + 1) * PAIR] = expand_table(table[h : h + 1, :])


GAIN = ((2, C, PAIR), F32)
BIAS = ((64, HEADS * PAIR), F32)
QKV_T = ((3 * C, AUG), BF16)
PROJ_T = ((C, C), BF16)
UP_T = ((HID, AUG), BF16)
DOWN = ((HID, C), BF16)
TABLE = ((8, 256), F32)
SMALL = [((2, 2, C), F32), ((2, 3 * C), F32), ((HEADS, 2, 225), F32), ((2, HID), F32)]
WEIGHTS = [((2, C, 3 * C), BF16), ((2, C, C), BF16), ((2, C, HID), BF16), ((2, C, HID), BF16)]
FIRST = [((C, 3 * C), BF16), ((C, C), BF16), ((C, HID), BF16), ((C, HID), BF16)]
TILE = ((TH, TW, C), BF16)


def lower_kernel(
    region,
    cot,
    norm_gains,
    qkv_bias,
    bias_table,
    up_bias,
    qkv_weight,
    proj_weight,
    up_weight,
    down_t,
    low_far,
    far_a,
    far_b,
    *rest,
):
    saves, rest = rest[: len(SAVES)], rest[len(SAVES) :]
    sems, field, table, gain, bias, tile, cot_tile, low, send_a, send_b, *rest = rest
    small, weights, kept = rest[:4], rest[4:8], rest[8:]
    sources = [norm_gains, qkv_bias, bias_table, up_bias]
    sources += [ref.at[0] for ref in (qkv_weight, proj_weight, up_weight, down_t)]
    copies = fetch(zip(sources + [region, cot], small + weights + [tile, cot_tile]), sems)
    w = Layers()
    finish(copies[:8])
    norm_gains, qkv_bias, bias_table, up_bias = small
    gain[0], gain[1] = wide_gains(norm_gains, 0)
    keep_bias(bias, table, bias_table, 0)
    w.gain, w.bias, w.down_t = PerLayer(gain), PerLayer(bias), PerLayer(weights[3])
    w.qkv_t = [augmented(weights[0][...], qkv_bias[0:1, :])]
    w.proj_t = [transposed(weights[1][...])]
    w.up_t = [augmented(weights[2][...], up_bias[0:1, :])]
    finish(copies[8:])
    x = [windows_t(tile, LOWER[2 * n : 2 * n + 2], 0, 0) for n in range(OWN_PAIRS)]
    leaving = []

    def keep(k, value):
        ref = kept[k]
        parts = per_heads(value) if ref.shape[2] == HEADS * PAIR else per_pair(value)
        for n, part in enumerate(parts):
            ref[n] = part.astype(ref.dtype)
        leaving.append(pltpu.make_async_copy(ref, saves[k], sems.at[13 + k]))
        leaving[-1].start()

    y, _ = forward(jnp.concatenate(x, 1), 0, w, None, keep)
    for n, part in enumerate(per_pair(y)):
        windows_back(part, field, LOWER[2 * n : 2 * n + 2])
    value = field[...].astype(BF16)
    low[...] = value
    top = jnp.concatenate([value[0:4], cot_tile[0:4]], 0)
    bottom = jnp.concatenate([value[TH - 4 :], cot_tile[TH - 4 :]], 0)
    near_part, far_part = to_sides(lax.axis_index("row"), top, bottom)
    send_a[...] = near_part
    send_b[...] = far_part
    leaving += fetch([(low, low_far), (send_a, far_a), (send_b, far_b)], sems.at[pl.ds(10, 3)])
    finish(leaving)


def prepare_kernel(
    after,
    norm_gains,
    qkv_bias,
    bias_table,
    up_bias,
    qkv_weight,
    proj_weight,
    up_weight,
    down_t,
    *rest,
):
    far, (sems, table), rest = rest[:8], rest[8:10], rest[10:]
    (qkv, proj, up, down_copy), small, made = rest[:4], rest[4:8], rest[8:]
    gain_0, gain_1, bias, qkv_t, proj_t, up_t, down_0, down_1 = made
    sources = [norm_gains, qkv_bias, bias_table, up_bias]
    sources += [qkv_weight, proj_weight, up_weight, down_t]
    finish(fetch(zip(sources, list(small) + [qkv, proj, up, down_copy]), sems))
    norm_gains, qkv_bias, bias_table, up_bias = small
    for b, gain in enumerate((gain_0, gain_1)):
        gain[0], gain[1] = wide_gains(norm_gains, b)
    keep_bias(bias, table, bias_table, 1)
    qkv_t[...] = augmented(qkv[1], qkv_bias[1:2, :])
    proj_t[...] = transposed(proj[1])
    up_t[...] = augmented(up[1], up_bias[1:2, :])
    down_0[...] = transposed(down_copy[0])
    down_1[...] = transposed(down_copy[1])
    finish(fetch(zip(made, far), sems))


PREPARED = [GAIN, GAIN, BIAS, QKV_T, PROJ_T, UP_T, DOWN, DOWN]


def strip_kernel(*refs):
    places, (send_a, send_b) = refs[:4], refs[4:]
    row = lax.axis_index("row")
    both = []
    for cols in (slice(0, 8), slice(TW - 8, TW)):
        strips = []
        for n, own in enumerate(places[:2]):
            above, below = sides(row, places[2][4 * n : 4 * n + 4], places[3][4 * n : 4 * n + 4])
            tall = [v.astype(F32) for v in (above[:, cols], own[:, cols], below[:, cols])]
            tall = jnp.concatenate(tall, 0)
            half = tall[:, 0:4] if cols.start == 0 else tall[:, 4:8]
            strips.append(jnp.concatenate([half[0:12], half[12:24]], 1))
        both.append(jnp.concatenate(strips, 0).astype(BF16))
    near_part, far_part = to_sides(lax.axis_index(COL_AXES), *both)
    send_a[...] = near_part
    send_b[...] = far_part


UPPER_IN = [TILE, TILE] + [((8, TW, C), BF16)] * 2 + [((24, 8, C), BF16)] * 2
UPPER_IN += WEIGHTS + PREPARED + SAVES


def upper_kernel(rows_cols, *rest):
    sources, rest = rest[: len(UPPER_IN)], rest[len(UPPER_IN) :]
    out_far, grad_far, keep_far, give_far, sems, out, grad_region, packed, *rest = rest
    local_in, rest = rest[: len(UPPER_IN)], rest[len(UPPER_IN) :]
    low_field, cot_field, out_field, grad_field, table, misc, *rest = rest
    d_gain, d_qkv, d_proj, d_up, d_down, d_bias = rest
    copies = fetch(zip(sources, local_in), sems)
    low, cot_tile = local_in[:2]
    got_row, got_col = local_in[2:4], local_in[4:6]
    prepared, saves = local_in[10:18], local_in[18:]

    w = Layers()
    w.qkv, w.proj, w.up, w.down_t = local_in[6:10]
    w.gain = PerLayer(*prepared[:2])
    w.bias, w.qkv_t, w.proj_t, w.up_t = [PerLayer(None, ref) for ref in prepared[2:6]]
    w.down = PerLayer(*prepared[6:])
    w.d_gain, w.d_qkv, w.d_proj = d_gain, d_qkv, d_proj
    w.d_up, w.d_down, w.d_bias = d_up, d_down, d_bias
    row, col = lax.axis_index("row"), lax.axis_index(COL_AXES)
    first_row, last_row = row == 0, row == rows_cols[0] - 1
    first_col, last_col = col == 0, col == rows_cols[1] - 1

    misc[...] = jnp.zeros(misc.shape, F32)
    table[...] = jnp.zeros(table.shape, F32)
    finish(copies[:6])
    left, right = sides(col, got_col[0][...].astype(F32), got_col[1][...].astype(F32))
    inner = slice(8, 8 + TW)
    for n, (field, own) in enumerate(((low_field, low), (cot_field, cot_tile))):
        part = slice(4 * n, 4 * n + 4)
        above, below = sides(row, got_row[0][part], got_row[1][part])
        field[0:4, inner, :] = above.astype(F32)
        field[4 : 4 + TH, inner, :] = own[...].astype(F32)
        field[4 + TH :, inner, :] = below.astype(F32)
        for half in range(2):
            rows = slice(12 * half, 12 * half + 12)
            from_rows, from_cols = slice(12 * n, 12 * n + 12), slice(4 * half, 4 * half + 4)
            field[rows, 4:8, :] = left[from_rows, from_cols, :]
            field[rows, 8 + TW : 12 + TW, :] = right[from_rows, from_cols, :]

    def edges(s):
        i, j = UPPER[s] if s < len(UPPER) else (1, 1)
        flags = (first_row, i == 0), (last_row, i == 2), (first_col, j == 0), (last_col, j == 6)
        return [jnp.where(flag, FAR, 0.0) if here else 0.0 for flag, here in flags]

    places = [UPPER[2 * n : 2 * n + 2] for n in range(UPPER_PAIRS)]
    key = lax.broadcasted_iota(jnp.int32, (64, PAIR), 0)
    first = lax.broadcasted_iota(jnp.int32, (64, PAIR), 1) < 64
    upper_half = (key // WIN) < 4
    left_half = (key % WIN) < 4
    penalty = []
    for n in range(UPPER_PAIRS):
        one, two = edges(2 * n), edges(2 * n + 1)
        if all(i == 1 and 0 < j < 6 for i, j in places[n]):
            penalty.append(None)
            continue
        top, bottom, before, after = [jnp.where(first, v, u) for v, u in zip(one, two)]
        penalty.append(jnp.where(upper_half, top, bottom) + jnp.where(left_half, before, after))
    slot = lax.broadcasted_iota(jnp.int32, (1, UPPER_PAIRS * PAIR), 1) // 64
    row_own = jnp.where(last_row, 1.0, 0.0)
    col_own = jnp.where(last_col, 1.0, 0.0)
    mask = jnp.where(
        slot < 12,
        1.0,
        jnp.where(
            slot < 18,
            row_own,
            jnp.where(slot < 19, row_own * col_own, jnp.where(slot < 21, col_own, 0.0)),
        ),
    )

    finish(copies[6:18])
    x = jnp.concatenate([windows_t(low_field, p, 0, 4) for p in places], 1)
    g = jnp.concatenate([windows_t(cot_field, p, 0, 4) for p in places], 1)
    y, saved = forward(x, 1, w, penalty)
    for p, part in zip(places, per_pair(y)):
        windows_back(part, out_field, p)
    out[...] = out_field[4 : 4 + TH, 4 : 4 + TW, :].astype(BF16)
    leaving = fetch([(out, out_far)], sems)
    dx = backward(g, 1, w, saved, mask)
    for p, part in zip(places, per_pair(dx)):
        windows_back(part, grad_field, p)

    g = jnp.concatenate([windows_t(grad_field, p, 4, 4) for p in places[:OWN_PAIRS]], 1)
    finish(copies[18:])
    saved = [jnp.concatenate([ref[n] for n in range(OWN_PAIRS)], 1) for ref in saves]
    dx = backward(g, 0, w, saved, None)
    for p, part in zip(places, per_pair(dx)):
        windows_back(part, grad_region, p)
    leaving += fetch([(grad_region, grad_far)], sems.at[pl.ds(1, 1)])

    for b in range(2):
        for j in range(3):
            lanes = slice(j * PAIR, (j + 1) * PAIR)
            packed[b, j * C : (j + 1) * C, :] = d_up[b, 0:C, lanes].astype(BF16)
            packed[b, 288 + j * C : 288 + (j + 1) * C, :] = d_down[b, :, lanes].astype(BF16)
            misc[b, 3 + j : 4 + j, :] = d_up[b, C : C + 1, lanes]
        for j in range(2):
            lanes = slice(j * PAIR, (j + 1) * PAIR)
            packed[b, 576 + j * C : 576 + (j + 1) * C, :] = d_qkv[b, 0:C, lanes].astype(BF16)
            misc[b, j : j + 1, :] = d_qkv[b, C : C + 1, lanes]
        last = jnp.concatenate([d_qkv[b, 0:C, 256:288], d_proj[b]], 1)
        packed[b, 768:864, :] = last.astype(BF16)
        misc[b, 2:3, 0:32] = d_qkv[b, C : C + 1, 256:288]
        for n in range(2):
            column = jnp.sum(jnp.transpose(d_gain[b, n]), 0, keepdims=True)
            misc[b, 6 + n : 7 + n, 0:C] = column
        for h in range(HEADS):
            table[h : h + 1, :] = fold_table(d_bias[b, :, h * PAIR : (h + 1) * PAIR])
        rows = reverse_lanes(table[...])
        misc[b, 8:16, :] = rows[:, 0:PAIR]
        misc[b, 16:24, :] = rows[:, PAIR:]
        packed[b, 864:896, :] = misc[b].astype(BF16)
        packed[b, 896:ROWS, :] = jnp.zeros((ROWS - 896, PAIR), BF16)
    core = lax.axis_index("core")
    pairs = [(packed.at[core], keep_far), (packed.at[1 - core], give_far)]
    finish(leaving + fetch(pairs, sems.at[pl.ds(2, 2)]))


def unpack_kernel(
    mine, other, gains, qkv, qkv_bias, table, proj, up, up_bias, down_t
):
    core = lax.axis_index("core")
    for b in range(2):
        flat = jnp.where(core == b, mine[...], other[...]).astype(F32)
        misc = flat[864:896]
        for j in range(3):
            lanes = slice(j * PAIR, (j + 1) * PAIR)
            up[b, :, lanes] = flat[j * C : (j + 1) * C]
            down_t[b, :, lanes] = flat[288 + j * C : 288 + (j + 1) * C]
            up_bias[b : b + 1, lanes] = misc[3 + j : 4 + j]
        for j in range(2):
            lanes = slice(j * PAIR, (j + 1) * PAIR)
            qkv[b, :, lanes] = flat[576 + j * C : 576 + (j + 1) * C]
            qkv_bias[b : b + 1, lanes] = misc[j : j + 1]
        last = flat[768:864]
        qkv[b, :, 256:288] = last[:, 0:32]
        proj[b] = last[:, 32:PAIR]
        qkv_bias[b : b + 1, 256:288] = misc[2:3, 0:32]
        for n in range(2):
            gains[b, n : n + 1, :] = misc[6 + n : 7 + n, 0:C]
        for h in range(HEADS):
            table[h, b : b + 1, 0:PAIR] = misc[8 + h : 9 + h]
            table[h, b : b + 1, PAIR:225] = misc[16 + h : 17 + h, 0:97]


def near(count):
    return [(i, i ^ 1) for i in range(count)]


def far(count):
    return [(i, ((i - 1) ^ 1) + 1) for i in range(1, count - 1)]


def swap(pair, axes, count):
    return lax.ppermute(pair[0], axes, near(count)), lax.ppermute(pair[1], axes, far(count))


def limited(size):
    return pltpu.CompilerParams(vmem_limit_bytes=size * 1024 * 1024)


def dma(count):
    return [pltpu.SemaphoreType.DMA((count,))]


def run_lower(*args):
    strip = ((8, TW, C), BF16)
    return pl.pallas_call(
        lower_kernel,
        out_shape=shapes([TILE, strip, strip] + SAVES),
        in_specs=[HBM] * 10,
        out_specs=[HBM] * (3 + len(SAVES)),
        scratch_shapes=dma(13 + len(SAVES))
        + scratch([((TH, TW, C), F32), TABLE, GAIN, BIAS, TILE, TILE, TILE, strip, strip])
        + scratch(SMALL + FIRST + SAVES),
        compiler_params=limited(60),
        name="lower",
    )(*args)


FLAT = ((ROWS, PAIR), BF16)


def run_upper(rows, cols, *args):
    wide = ((TH + 8, TW + 16, C), F32)
    narrow = ((TH + 8, TW + 8, C), F32)
    sums = [
        ((2, 2, C, PAIR), F32),
        ((2, AUG, 3 * C), F32),
        ((2, C, C), F32),
        ((2, AUG, HID), F32),
        ((2, C, HID), F32),
        ((2, 64, HEADS * PAIR), F32),
    ]
    results = [TILE, ((TH, TW, C), F32)]
    return pl.pallas_call(
        functools.partial(upper_kernel, (rows, cols)),
        out_shape=shapes(results + [FLAT, FLAT]),
        in_specs=[HBM] * len(UPPER_IN),
        out_specs=[HBM] * 4,
        scratch_shapes=dma(len(UPPER_IN))
        + scratch(results + [((2, ROWS, PAIR), BF16)] + UPPER_IN + [wide, wide, narrow, narrow, TABLE, ((2, 32, PAIR), F32)] + sums),
        compiler_params=limited(60),
        name="upper",
    )(*args)


def body(region, cotangent, gains, qkv, qkv_bias, table, proj, up, up_bias, down):
    rows, cols = lax.axis_size("row"), lax.axis_size(COL_AXES)
    table_t = jnp.transpose(table, (1, 0, 2))
    down_t = jnp.transpose(down, (0, 2, 1))
    params = (gains, qkv_bias, table_t, up_bias, qkv, proj, up, down_t)
    low, send_a, send_b, *saved = run_lower(region, cotangent, *params)
    row_got = swap((send_a, send_b), "row", rows)
    prepared = pl.pallas_call(
        prepare_kernel,
        out_shape=shapes(PREPARED),
        in_specs=[HBM] * 9,
        out_specs=[HBM] * len(PREPARED),
        scratch_shapes=dma(8) + scratch([TABLE] + WEIGHTS + SMALL + PREPARED),
        compiler_params=limited(60),
        cost_estimate=pl.CostEstimate(flops=10**9, bytes_accessed=4 * 10**6, transcendentals=0),
        name="prepare",
    )(saved[1], *params)
    strip = ((24, 8, C), BF16)
    send = pl.pallas_call(
        strip_kernel,
        out_shape=shapes([strip, strip]),
        in_specs=[VMEM] * 4,
        out_specs=[VMEM] * 2,
        compiler_params=limited(8),
        name="strips",
    )(low, cotangent, *row_got)
    col_got = swap(send, COL_AXES, cols)
    out, grad_region, keep, give = run_upper(
        rows, cols, low, cotangent, *row_got, *col_got, qkv, proj, up, down_t, *prepared, *saved
    )
    got = lax.ppermute(give, "core", near(2))
    share = (keep.astype(F32) + got.astype(F32)).astype(BF16).reshape(PEERS, -1, PAIR)
    peers = ("row", "col_half")
    parts = lax.all_to_all(share, peers, 0, 0)
    part = jnp.sum(parts.astype(F32), 0, keepdims=True).astype(BF16)
    mine = lax.all_to_all(jnp.broadcast_to(part, share.shape), peers, 0, 0)
    mine = mine.reshape(ROWS, PAIR)
    other = lax.ppermute(mine, "core", near(2))
    grads = pl.pallas_call(
        unpack_kernel,
        out_shape=tuple(
            jax.ShapeDtypeStruct(shape, F32)
            for shape in (
                (2, 2, C),
                (2, C, 3 * C),
                (2, 3 * C),
                (HEADS, 2, 225),
                (2, C, C),
                (2, C, HID),
                (2, HID),
                (2, C, HID),
            )
        ),
        in_specs=[VMEM] * 2,
        out_specs=[VMEM] * 8,
        compiler_params=limited(8),
        name="unpack",
    )(mine, other)
    d_gains, d_qkv, d_qkv_bias, d_table, d_proj, d_up, d_up_bias, d_down_t = grads
    return (
        out,
        grad_region,
        d_gains,
        d_qkv,
        d_qkv_bias,
        jnp.transpose(d_table, (1, 0, 2)),
        d_proj,
        d_up,
        d_up_bias,
        jnp.transpose(d_down_t, (0, 2, 1)),
    )


def solution(mesh):
    rows, cols = mesh.devices.shape
    fine = Mesh(mesh.devices.reshape(rows, cols // 2, 2), ("row", "col_half", "core"))
    tile = P("row", ("col_half", "core"), None)
    return jax.shard_map(
        body,
        mesh=fine,
        in_specs=(tile, tile) + (P(),) * 8,
        out_specs=(tile, tile) + (P(),) * 8,
        check_vma=False,
    )
```

```python
import functools

import jax
import jax.numpy as jnp
from jax import lax
from jax.experimental import pallas as pl
from jax.experimental.pallas import tpu as pltpu
from jax.sharding import Mesh
from jax.sharding import PartitionSpec as P

C = 96
HEADS = 3
HEAD = 32
HID = 384
WIN = 8
TH = 16
TW = 48
AUG = 112
PAIR = 128
ROWS = 1024
PEERS = 128
LOG2E = 1.4426950408889634
SCALE = HEAD**-0.5
FAR = -1e30
F32 = jnp.float32
BF16 = jnp.bfloat16

LOWER = [(i, j) for i in (0, 1) for j in range(6)]
UPPER = LOWER + [(2, j) for j in range(7)] + [(0, 6), (1, 6)]
OWN_PAIRS = 6
UPPER_PAIRS = 11
CHUNK = 2
EARLY = 9
FEED = 256


def dot(a, b):
    return jnp.dot(a, b, preferred_element_type=F32)


def dot_nt(a, b):
    return lax.dot_general(a, b, (((1,), (1,)), ((), ())), preferred_element_type=F32)


def split3(v):
    hi = v.astype(BF16)
    rest = v - hi.astype(F32)
    mid = rest.astype(BF16)
    return hi, mid, (rest - mid.astype(F32)).astype(BF16)


def transposed(v):
    return jnp.transpose(v.astype(F32)).astype(BF16)


def augmented(weight, bias):
    hi, mid, lo = split3(bias)
    rows = lax.broadcasted_iota(jnp.int32, (AUG - C, bias.shape[1]), 0)
    extra = jnp.where(
        rows == 0,
        hi.astype(F32),
        jnp.where(rows == 1, mid.astype(F32), jnp.where(rows == 2, lo.astype(F32), 0.0)),
    )
    return transposed(jnp.concatenate([weight.astype(F32), extra], 0))


def lane_code(lanes):
    token = lanes % 64
    return (token // WIN) * 15 + token % WIN


def expand_table(row):
    parts = []
    for kr in range(WIN):
        wide = jnp.broadcast_to(row, (WIN, 256))
        parts.append(pltpu.roll(wide, (15 * kr - 112) % 256, 1, stride=1, stride_axis=0))
    rolled = jnp.concatenate(parts, 0)
    lane = lax.broadcasted_iota(jnp.int32, (256, PAIR), 0)
    query = lax.broadcasted_iota(jnp.int32, (256, PAIR), 1)
    onehot = (lane == lane_code(query)).astype(BF16)
    hi, mid, lo = split3(rolled)
    return (dot(hi, onehot) + dot(mid, onehot) + dot(lo, onehot)) * LOG2E


def fold_table(acc):
    lane = lax.broadcasted_iota(jnp.int32, (PAIR, 256), 1)
    query = lax.broadcasted_iota(jnp.int32, (PAIR, 256), 0)
    onehot = (lane == 112 - lane_code(query)).astype(BF16)
    hi, mid, _ = split3(acc)
    wide = dot(hi, onehot) + dot(mid, onehot)
    total = jnp.zeros((WIN, 256), F32)
    for kr in range(WIN):
        total += pltpu.roll(
            wide[kr * WIN : (kr + 1) * WIN], 15 * kr, 1, stride=1, stride_axis=0
        )
    return jnp.sum(total, 0, keepdims=True)


def reverse_lanes(rows):
    a = lax.broadcasted_iota(jnp.int32, (256, 256), 0)
    b = lax.broadcasted_iota(jnp.int32, (256, 256), 1)
    onehot = (a + b == 224).astype(BF16)
    hi, mid, _ = split3(rows)
    return dot(hi, onehot) + dot(mid, onehot)


def norm(x):
    mean = jnp.sum(x, 0, keepdims=True) * (1.0 / C)
    centred = x - mean
    var = jnp.sum(centred * centred, 0, keepdims=True) * (1.0 / C)
    r = lax.rsqrt(var + 1e-05)
    return centred * r, r


def norm_back(dxhat, xhat, r):
    m1 = jnp.sum(dxhat, 0, keepdims=True) * (1.0 / C)
    m2 = jnp.sum(dxhat * xhat, 0, keepdims=True) * (1.0 / C)
    return r * (dxhat - m1 - xhat * m2)


def per_pair(v):
    return [v[:, p : p + PAIR] for p in range(0, v.shape[1], PAIR)]


def per_heads(v):
    step = HEADS * PAIR
    return [v[:, p : p + step] for p in range(0, v.shape[1], step)]


def split_lanes(v):
    return [v[:, p : p + FEED] for p in range(0, v.shape[1], FEED)]


def scaled(v, gain):
    return jnp.concatenate([part * gain for part in per_pair(v)], 1)


def with_ones(v):
    return jnp.concatenate([v, jnp.ones((AUG - C, v.shape[1]), BF16)], 0)


def head_blocks(v):
    zero = jnp.zeros((HEAD, PAIR), v.dtype)
    cols = []
    for h in range(HEADS):
        rows = [v[g * HEAD : (g + 1) * HEAD] if g == h else zero for g in range(HEADS)]
        cols.append(jnp.concatenate(rows, 0))
    return jnp.concatenate(cols, 1)


def first_lanes(v):
    lane = lax.broadcasted_iota(jnp.int32, (1, v.shape[1]), 1)
    return (lane % PAIR) < 64


def window_rows(v):
    zero = jnp.zeros_like(v)
    first = jnp.broadcast_to(first_lanes(v), v.shape)
    return jnp.concatenate([jnp.where(first, v, zero), jnp.where(first, zero, v)], 0)


def deep_rows(v):
    pad = jnp.zeros((PAIR - C, HEADS * PAIR), v.dtype)
    return window_rows(jnp.concatenate([head_blocks(v), pad], 0))


def deep_tokens(v):
    pad = jnp.zeros((PAIR - C, PAIR), v.dtype)
    tokens = transposed(jnp.concatenate([v, pad], 0))
    return jnp.concatenate([tokens[:64], tokens[64:]], 1)


def by_head(rows, blocks, product):
    return jnp.concatenate(
        [
            product(rows[h * HEAD : (h + 1) * HEAD], blocks[:, h * PAIR : (h + 1) * PAIR])
            for h in range(HEADS)
        ],
        0,
    )


def gelu_parts(u):
    k = 0.7978845608028654
    uu = u * u
    half = 0.5 + 0.5 * jnp.tanh(u * (k + (k * 0.044715) * uu))
    m = u * half
    return m, half + m * (1.0 - half) * (2 * k + (6 * k * 0.044715) * uu)


def forward(x, b, w, penalty, keep=lambda n, v: None):
    xhat1, r1 = norm(x)
    keep(0, xhat1)
    keep(1, r1)
    a = with_ones(scaled(xhat1, w.gain[b, 0]).astype(BF16))
    keep(2, a)
    qkv = dot(w.qkv_t[b], a).astype(BF16)
    keep(3, qkv)
    parts = per_pair(qkv)
    scores = [dot(deep_tokens(part[C : 2 * C]), deep_rows(part[:C])) for part in parts]
    probs = []
    for p in range(0, len(parts), CHUNK):
        some = range(p, min(p + CHUNK, len(parts)))
        bias = jnp.concatenate([w.bias[b]] * len(some), 1)
        score = jnp.concatenate([scores[q] for q in some], 1) * (SCALE * LOG2E) + bias
        if penalty is not None:
            none = jnp.zeros((64, PAIR), F32)
            extra = [none if penalty[q] is None else penalty[q] for q in some]
            score = score + jnp.concatenate([v for v in extra for _ in range(HEADS)], 1)
        e = jnp.exp2(score - jnp.max(score, 0, keepdims=True))
        probs.append((e * (1.0 / jnp.sum(e, 0, keepdims=True))).astype(BF16))
    probs = jnp.concatenate(probs, 1)
    keep(4, probs)
    mixed = [
        by_head(part[2 * C :], window_rows(prob), dot)
        for part, prob in zip(parts, per_heads(probs))
    ]
    mix = jnp.concatenate(mixed, 1).astype(BF16)
    keep(5, mix)
    h = x + dot(w.proj_t[b], mix)
    xhat2, r2 = norm(h)
    keep(6, xhat2)
    keep(7, r2)
    f = with_ones(scaled(xhat2, w.gain[b, 1]).astype(BF16))
    keep(8, f)
    m, slope = [], []
    for part in split_lanes(f):
        one, two = gelu_parts(dot(w.up_t[b], part))
        m.append(one.astype(BF16))
        slope.append(two.astype(BF16))
    m, slope = jnp.concatenate(m, 1), jnp.concatenate(slope, 1)
    keep(9, m)
    keep(10, slope)
    out = h + dot(w.down_t[b], m)
    return out, (xhat1, r1, a, qkv, probs, mix, xhat2, r2, f, m, slope)


def backward(g, b, w, saved, mask):
    xhat1, r1, a, qkv, probs, mix, xhat2, r2, f, m, slope = saved

    def own(v):
        return v if mask is None else v * mask.astype(v.dtype)

    def pairs_sum(v):
        return sum(per_pair(v))

    g16 = g.astype(BF16)
    du = []
    for part, part_slope in zip(split_lanes(g16), split_lanes(slope)):
        du.append((dot(w.down[b], part) * part_slope.astype(F32)).astype(BF16))
    du = jnp.concatenate(du, 1)
    w.d_down[b] = dot_nt(own(g16), m)
    w.d_up[b] = dot_nt(own(f), du)
    df = dot(w.up[b], du)
    w.d_gain[b, 1] = pairs_sum(own(df * xhat2))
    dh = g + norm_back(scaled(df, w.gain[b, 1]), xhat2, r2)
    dh16 = dh.astype(BF16)
    w.d_proj[b] = dot_nt(mix, own(dh16))
    dmix = dot(w.proj[b], dh16).astype(BF16)
    parts, d_parts = per_pair(qkv), per_pair(dmix)
    dprobs = [dot(deep_tokens(v[2 * C :]), deep_rows(d)) for v, d in zip(parts, d_parts)]
    ds16 = []
    d_bias = None
    for p in range(0, len(parts), CHUNK):
        some = range(p, min(p + CHUNK, len(parts)))
        prob = probs[:, HEADS * PAIR * p : HEADS * PAIR * (p + len(some))].astype(F32)
        weighted = prob * jnp.concatenate([dprobs[q] for q in some], 1)
        ds = weighted - prob * jnp.sum(weighted, 0, keepdims=True)
        ds16.append(ds.astype(BF16))
        for q, part in zip(some, per_heads(ds)):
            if mask is not None:
                part = part * jnp.concatenate([per_pair(mask)[q]] * HEADS, 1)
            d_bias = part if d_bias is None else d_bias + part
    w.d_bias[b] = d_bias
    dq, dk, dv = [], [], []
    ds16 = jnp.concatenate(ds16, 1)
    for part, d_part, prob, ds in zip(parts, d_parts, per_heads(probs), per_heads(ds16)):
        ds = window_rows(ds)
        dv.append(by_head(d_part, window_rows(prob), dot_nt))
        dk.append(by_head(part[:C], ds, dot_nt) * SCALE)
        dq.append(by_head(part[C : 2 * C], ds, dot) * SCALE)
    dqkv = jnp.concatenate([jnp.concatenate(v, 1) for v in (dq, dk, dv)], 0).astype(BF16)
    w.d_qkv[b] = dot_nt(own(a), dqkv)
    da = dot(w.qkv[b], dqkv)
    w.d_gain[b, 0] = pairs_sum(own(da * xhat1))
    return dh + norm_back(scaled(da, w.gain[b, 0]), xhat1, r1)


class Layers:
    pass


class PerLayer:
    def __init__(self, *refs):
        self.refs = refs

    def __getitem__(self, key):
        if isinstance(key, tuple):
            return self.refs[key[0]][key[1]]
        return self.refs[key][...]


def fetch(pairs, sems):
    copies = [pltpu.make_async_copy(src, dst, sems.at[n]) for n, (src, dst) in enumerate(pairs)]
    for copy in copies:
        copy.start()
    return copies


def finish(copies):
    for copy in copies:
        copy.wait()


def windows_t(ref, places, r0, c0):
    tokens = []
    for i, j in places:
        block = ref[r0 + WIN * i : r0 + WIN * (i + 1), c0 + WIN * j : c0 + WIN * (j + 1), :]
        tokens.append(block.astype(F32).reshape(WIN * WIN, C))
    if len(tokens) == 1:
        tokens.append(jnp.zeros((WIN * WIN, C), F32))
    return jnp.transpose(jnp.concatenate(tokens, 0))


def windows_back(value, ref, places):
    tokens = jnp.transpose(value)
    for n, (i, j) in enumerate(places):
        block = tokens[n * 64 : (n + 1) * 64].reshape(WIN, WIN, C)
        ref[WIN * i : WIN * (i + 1), WIN * j : WIN * (j + 1), :] = block.astype(ref.dtype)


VMEM = pl.BlockSpec(memory_space=pltpu.VMEM)
HBM = pl.BlockSpec(memory_space=pltpu.HBM)
COL_AXES = ("col_half", "core")
SAVES = [
    ((OWN_PAIRS, C, PAIR), F32),
    ((OWN_PAIRS, 1, PAIR), F32),
    ((OWN_PAIRS, AUG, PAIR), BF16),
    ((OWN_PAIRS, 3 * C, PAIR), BF16),
    ((OWN_PAIRS, 64, HEADS * PAIR), BF16),
    ((OWN_PAIRS, C, PAIR), BF16),
    ((OWN_PAIRS, C, PAIR), F32),
    ((OWN_PAIRS, 1, PAIR), F32),
    ((OWN_PAIRS, AUG, PAIR), BF16),
    ((OWN_PAIRS, HID, PAIR), BF16),
    ((OWN_PAIRS, HID, PAIR), BF16),
]


def shapes(entries):
    return [jax.ShapeDtypeStruct(shape, kind) for shape, kind in entries]


def scratch(entries):
    return [pltpu.VMEM(shape, kind) for shape, kind in entries]


def sides(position, from_a, from_b):
    even = position % 2 == 0
    return jnp.where(even, from_b, from_a), jnp.where(even, from_a, from_b)


def to_sides(position, before, after):
    even = position % 2 == 0
    return jnp.where(even, after, before), jnp.where(even, before, after)


def wide_gains(norm_gains, b):
    rows = [jnp.broadcast_to(norm_gains[b, n : n + 1, :], (PAIR, C)) for n in range(2)]
    return [jnp.transpose(row) for row in rows]


def keep_bias(bias, table, bias_table, b):
    table[...] = jnp.zeros(table.shape, F32)
    for h in range(HEADS):
        table[h : h + 1, 0 : bias_table.shape[2]] = bias_table[h, b : b + 1, :]
        bias[:, h * PAIR : (h + 1) * PAIR] = expand_table(table[h : h + 1, :])


GAIN = ((2, C, PAIR), F32)
BIAS = ((64, HEADS * PAIR), F32)
QKV_T = ((3 * C, AUG), BF16)
PROJ_T = ((C, C), BF16)
UP_T = ((HID, AUG), BF16)
DOWN = ((HID, C), BF16)
TABLE = ((8, 256), F32)
SMALL = [((2, 2, C), F32), ((2, 3 * C), F32), ((HEADS, 2, 225), F32), ((2, HID), F32)]
WEIGHTS = [((2, C, 3 * C), BF16), ((2, C, C), BF16), ((2, C, HID), BF16), ((2, C, HID), BF16)]
FIRST = [((C, 3 * C), BF16), ((C, C), BF16), ((C, HID), BF16), ((C, HID), BF16)]
TILE = ((TH, TW, C), BF16)


def lower_kernel(
    region,
    cot,
    norm_gains,
    qkv_bias,
    bias_table,
    up_bias,
    qkv_weight,
    proj_weight,
    up_weight,
    down_t,
    low_far,
    far_a,
    far_b,
    *rest,
):
    saves, rest = rest[:EARLY], rest[EARLY:]
    sems, field, table, gain, bias, tile, cot_tile, low, send_a, send_b, *rest = rest
    small, weights, kept = rest[:4], rest[4:8], rest[8:]
    sources = [norm_gains, qkv_bias, bias_table, up_bias]
    sources += [ref.at[0] for ref in (qkv_weight, proj_weight, up_weight, down_t)]
    copies = fetch(zip(sources + [region, cot], small + weights + [tile, cot_tile]), sems)
    w = Layers()
    finish(copies[:8])
    norm_gains, qkv_bias, bias_table, up_bias = small
    gain[0], gain[1] = wide_gains(norm_gains, 0)
    keep_bias(bias, table, bias_table, 0)
    w.gain, w.bias, w.down_t = PerLayer(gain), PerLayer(bias), PerLayer(weights[3])
    w.qkv_t = [augmented(weights[0][...], qkv_bias[0:1, :])]
    w.proj_t = [transposed(weights[1][...])]
    w.up_t = [augmented(weights[2][...], up_bias[0:1, :])]
    finish(copies[8:])
    x = [windows_t(tile, LOWER[2 * n : 2 * n + 2], 0, 0) for n in range(OWN_PAIRS)]
    leaving = []

    def keep(k, value):
        if k >= EARLY:
            return
        ref = kept[k]
        parts = per_heads(value) if ref.shape[2] == HEADS * PAIR else per_pair(value)
        for n, part in enumerate(parts):
            ref[n] = part.astype(ref.dtype)
        leaving.append(pltpu.make_async_copy(ref, saves[k], sems.at[13 + k]))
        leaving[-1].start()

    y, _ = forward(jnp.concatenate(x, 1), 0, w, None, keep)
    for n, part in enumerate(per_pair(y)):
        windows_back(part, field, LOWER[2 * n : 2 * n + 2])
    value = field[...].astype(BF16)
    low[...] = value
    top = jnp.concatenate([value[0:4], cot_tile[0:4]], 0)
    bottom = jnp.concatenate([value[TH - 4 :], cot_tile[TH - 4 :]], 0)
    near_part, far_part = to_sides(lax.axis_index("row"), top, bottom)
    send_a[...] = near_part
    send_b[...] = far_part
    leaving += fetch([(low, low_far), (send_a, far_a), (send_b, far_b)], sems.at[pl.ds(10, 3)])
    finish(leaving)


def prepare_kernel(
    feed,
    norm_gains,
    qkv_bias,
    bias_table,
    up_bias,
    qkv_weight,
    proj_weight,
    up_weight,
    down_t,
    *rest,
):
    far, (sems, table, f), rest = rest[:10], rest[10:13], rest[13:]
    (qkv, proj, up, down_copy), small, made = rest[:4], rest[4:8], rest[8:]
    gain_0, gain_1, bias, qkv_t, proj_t, up_t, down_0, down_1, m, slope = made
    sources = [norm_gains, qkv_bias, bias_table, up_bias]
    sources += [qkv_weight, proj_weight, up_weight, down_t]
    finish(fetch(zip([feed] + sources, [f, *small, qkv, proj, up, down_copy]), sems))
    norm_gains, qkv_bias, bias_table, up_bias = small
    lower_up_t = augmented(up[0], up_bias[0:1, :])
    for n in range(OWN_PAIRS):
        one, two = gelu_parts(dot(lower_up_t, f[n]))
        m[n] = one.astype(BF16)
        slope[n] = two.astype(BF16)
    leaving = fetch([(m, far[8]), (slope, far[9])], sems.at[pl.ds(8, 2)])
    for b, gain in enumerate((gain_0, gain_1)):
        gain[0], gain[1] = wide_gains(norm_gains, b)
    keep_bias(bias, table, bias_table, 1)
    qkv_t[...] = augmented(qkv[1], qkv_bias[1:2, :])
    proj_t[...] = transposed(proj[1])
    up_t[...] = augmented(up[1], up_bias[1:2, :])
    down_0[...] = transposed(down_copy[0])
    down_1[...] = transposed(down_copy[1])
    finish(leaving + fetch(zip(made[:8], far), sems))


PREPARED = [GAIN, GAIN, BIAS, QKV_T, PROJ_T, UP_T, DOWN, DOWN]


SIDE_COLUMNS = (slice(0, 8), slice(TW - 8, TW))


def own_kernel(low, cot, own):
    for side, cols in enumerate(SIDE_COLUMNS):
        own[side, 0] = low[:, cols]
        own[side, 1] = cot[:, cols]


def strip_kernel(own, row_a, row_b, send_a, send_b):
    row = lax.axis_index("row")
    both = []
    for side, cols in enumerate(SIDE_COLUMNS):
        strips = []
        for n in range(2):
            above, below = sides(row, row_a[4 * n : 4 * n + 4], row_b[4 * n : 4 * n + 4])
            tall = [v.astype(F32) for v in (above[:, cols], own[side, n], below[:, cols])]
            tall = jnp.concatenate(tall, 0)
            half = tall[:, 0:4] if cols.start == 0 else tall[:, 4:8]
            strips.append(jnp.concatenate([half[0:12], half[12:24]], 1))
        both.append(jnp.concatenate(strips, 0).astype(BF16))
    near_part, far_part = to_sides(lax.axis_index(COL_AXES), *both)
    send_a[...] = near_part
    send_b[...] = far_part


UPPER_IN = [TILE, TILE] + [((8, TW, C), BF16)] * 2 + [((24, 8, C), BF16)] * 2
UPPER_IN += WEIGHTS + PREPARED + SAVES


def upper_kernel(rows_cols, *rest):
    sources, rest = rest[: len(UPPER_IN)], rest[len(UPPER_IN) :]
    out_far, grad_far, keep_far, give_far, sems, out, grad_region, packed, *rest = rest
    local_in, rest = rest[: len(UPPER_IN)], rest[len(UPPER_IN) :]
    low_field, cot_field, out_field, grad_field, table, misc, *rest = rest
    d_gain, d_qkv, d_proj, d_up, d_down, d_bias = rest
    copies = fetch(zip(sources, local_in), sems)
    low, cot_tile = local_in[:2]
    got_row, got_col = local_in[2:4], local_in[4:6]
    prepared, saves = local_in[10:18], local_in[18:]

    w = Layers()
    w.qkv, w.proj, w.up, w.down_t = local_in[6:10]
    w.gain = PerLayer(*prepared[:2])
    w.bias, w.qkv_t, w.proj_t, w.up_t = [PerLayer(None, ref) for ref in prepared[2:6]]
    w.down = PerLayer(*prepared[6:])
    w.d_gain, w.d_qkv, w.d_proj = d_gain, d_qkv, d_proj
    w.d_up, w.d_down, w.d_bias = d_up, d_down, d_bias
    row, col = lax.axis_index("row"), lax.axis_index(COL_AXES)
    first_row, last_row = row == 0, row == rows_cols[0] - 1
    first_col, last_col = col == 0, col == rows_cols[1] - 1

    misc[...] = jnp.zeros(misc.shape, F32)
    table[...] = jnp.zeros(table.shape, F32)
    finish(copies[:6])
    left, right = sides(col, got_col[0][...].astype(F32), got_col[1][...].astype(F32))
    inner = slice(8, 8 + TW)
    for n, (field, own) in enumerate(((low_field, low), (cot_field, cot_tile))):
        part = slice(4 * n, 4 * n + 4)
        above, below = sides(row, got_row[0][part], got_row[1][part])
        field[0:4, inner, :] = above.astype(F32)
        field[4 : 4 + TH, inner, :] = own[...].astype(F32)
        field[4 + TH :, inner, :] = below.astype(F32)
        for half in range(2):
            rows = slice(12 * half, 12 * half + 12)
            from_rows, from_cols = slice(12 * n, 12 * n + 12), slice(4 * half, 4 * half + 4)
            field[rows, 4:8, :] = left[from_rows, from_cols, :]
            field[rows, 8 + TW : 12 + TW, :] = right[from_rows, from_cols, :]

    def edges(s):
        i, j = UPPER[s] if s < len(UPPER) else (1, 1)
        flags = (first_row, i == 0), (last_row, i == 2), (first_col, j == 0), (last_col, j == 6)
        return [jnp.where(flag, FAR, 0.0) if here else 0.0 for flag, here in flags]

    places = [UPPER[2 * n : 2 * n + 2] for n in range(UPPER_PAIRS)]
    key = lax.broadcasted_iota(jnp.int32, (64, PAIR), 0)
    first = lax.broadcasted_iota(jnp.int32, (64, PAIR), 1) < 64
    upper_half = (key // WIN) < 4
    left_half = (key % WIN) < 4
    penalty = []
    for n in range(UPPER_PAIRS):
        one, two = edges(2 * n), edges(2 * n + 1)
        if all(i == 1 and 0 < j < 6 for i, j in places[n]):
            penalty.append(None)
            continue
        top, bottom, before, after = [jnp.where(first, v, u) for v, u in zip(one, two)]
        penalty.append(jnp.where(upper_half, top, bottom) + jnp.where(left_half, before, after))
    slot = lax.broadcasted_iota(jnp.int32, (1, UPPER_PAIRS * PAIR), 1) // 64
    row_own = jnp.where(last_row, 1.0, 0.0)
    col_own = jnp.where(last_col, 1.0, 0.0)
    mask = jnp.where(
        slot < 12,
        1.0,
        jnp.where(
            slot < 18,
            row_own,
            jnp.where(slot < 19, row_own * col_own, jnp.where(slot < 21, col_own, 0.0)),
        ),
    )

    finish(copies[6:18])
    x = jnp.concatenate([windows_t(low_field, p, 0, 4) for p in places], 1)
    g = jnp.concatenate([windows_t(cot_field, p, 0, 4) for p in places], 1)
    y, saved = forward(x, 1, w, penalty)
    for p, part in zip(places, per_pair(y)):
        windows_back(part, out_field, p)
    out[...] = out_field[4 : 4 + TH, 4 : 4 + TW, :].astype(BF16)
    leaving = fetch([(out, out_far)], sems)
    dx = backward(g, 1, w, saved, mask)
    for p, part in zip(places, per_pair(dx)):
        windows_back(part, grad_field, p)

    g = jnp.concatenate([windows_t(grad_field, p, 4, 4) for p in places[:OWN_PAIRS]], 1)
    finish(copies[18:])
    def pack(b):
        for j in range(3):
            lanes = slice(j * PAIR, (j + 1) * PAIR)
            packed[b, j * C : (j + 1) * C, :] = d_up[b, 0:C, lanes].astype(BF16)
            packed[b, 288 + j * C : 288 + (j + 1) * C, :] = d_down[b, :, lanes].astype(BF16)
            misc[b, 3 + j : 4 + j, :] = d_up[b, C : C + 1, lanes]
        for j in range(2):
            lanes = slice(j * PAIR, (j + 1) * PAIR)
            packed[b, 576 + j * C : 576 + (j + 1) * C, :] = d_qkv[b, 0:C, lanes].astype(BF16)
            misc[b, j : j + 1, :] = d_qkv[b, C : C + 1, lanes]
        last = jnp.concatenate([d_qkv[b, 0:C, 256:288], d_proj[b]], 1)
        packed[b, 768:864, :] = last.astype(BF16)
        misc[b, 2:3, 0:32] = d_qkv[b, C : C + 1, 256:288]
        for n in range(2):
            column = jnp.sum(jnp.transpose(d_gain[b, n]), 0, keepdims=True)
            misc[b, 6 + n : 7 + n, 0:C] = column
        for h in range(HEADS):
            table[h : h + 1, :] = fold_table(d_bias[b, :, h * PAIR : (h + 1) * PAIR])
        rows = reverse_lanes(table[...])
        misc[b, 8:16, :] = rows[:, 0:PAIR]
        misc[b, 16:24, :] = rows[:, PAIR:]
        packed[b, 864:896, :] = misc[b].astype(BF16)
        packed[b, 896:ROWS, :] = jnp.zeros((ROWS - 896, PAIR), BF16)

    saved = [jnp.concatenate([ref[n] for n in range(OWN_PAIRS)], 1) for ref in saves]
    dx = backward(g, 0, w, saved, None)
    for p, part in zip(places, per_pair(dx)):
        windows_back(part, grad_region, p)
    leaving += fetch([(grad_region, grad_far)], sems.at[pl.ds(1, 1)])

    pack(0)
    pack(1)
    core = lax.axis_index("core")
    pairs = [(packed.at[core], keep_far), (packed.at[1 - core], give_far)]
    finish(leaving + fetch(pairs, sems.at[pl.ds(2, 2)]))


def unpack_kernel(
    mine, other, gains, qkv, qkv_bias, table, proj, up, up_bias, down_t
):
    core = lax.axis_index("core")
    for b in range(2):
        flat = jnp.where(core == b, mine[...], other[...]).astype(F32)
        misc = flat[864:896]
        for j in range(3):
            lanes = slice(j * PAIR, (j + 1) * PAIR)
            up[b, :, lanes] = flat[j * C : (j + 1) * C]
            down_t[b, :, lanes] = flat[288 + j * C : 288 + (j + 1) * C]
            up_bias[b : b + 1, lanes] = misc[3 + j : 4 + j]
        for j in range(2):
            lanes = slice(j * PAIR, (j + 1) * PAIR)
            qkv[b, :, lanes] = flat[576 + j * C : 576 + (j + 1) * C]
            qkv_bias[b : b + 1, lanes] = misc[j : j + 1]
        last = flat[768:864]
        qkv[b, :, 256:288] = last[:, 0:32]
        proj[b] = last[:, 32:PAIR]
        qkv_bias[b : b + 1, 256:288] = misc[2:3, 0:32]
        for n in range(2):
            gains[b, n : n + 1, :] = misc[6 + n : 7 + n, 0:C]
        for h in range(HEADS):
            table[h, b : b + 1, 0:PAIR] = misc[8 + h : 9 + h]
            table[h, b : b + 1, PAIR:225] = misc[16 + h : 17 + h, 0:97]


def near(count):
    return [(i, i ^ 1) for i in range(count)]


def far(count):
    return [(i, ((i - 1) ^ 1) + 1) for i in range(1, count - 1)]


def swap(pair, axes, count):
    second = lax.ppermute(pair[1], axes, far(count))
    return lax.ppermute(pair[0], axes, near(count)), second


def limited(size):
    return pltpu.CompilerParams(vmem_limit_bytes=size * 1024 * 1024)


def dma(count):
    return [pltpu.SemaphoreType.DMA((count,))]


def run_lower(*args):
    strip = ((8, TW, C), BF16)
    return pl.pallas_call(
        lower_kernel,
        out_shape=shapes([TILE, strip, strip] + SAVES[:EARLY]),
        in_specs=[HBM] * 10,
        out_specs=[HBM] * (3 + EARLY),
        scratch_shapes=dma(13 + EARLY)
        + scratch([((TH, TW, C), F32), TABLE, GAIN, BIAS, TILE, TILE, TILE, strip, strip])
        + scratch(SMALL + FIRST + SAVES[:EARLY]),
        compiler_params=limited(60),
        name="lower",
    )(*args)


FLAT = ((ROWS, PAIR), BF16)


def run_upper(rows, cols, *args):
    wide = ((TH + 8, TW + 16, C), F32)
    narrow = ((TH + 8, TW + 8, C), F32)
    sums = [
        ((2, 2, C, PAIR), F32),
        ((2, AUG, 3 * C), F32),
        ((2, C, C), F32),
        ((2, AUG, HID), F32),
        ((2, C, HID), F32),
        ((2, 64, HEADS * PAIR), F32),
    ]
    results = [TILE, ((TH, TW, C), F32)]
    return pl.pallas_call(
        functools.partial(upper_kernel, (rows, cols)),
        out_shape=shapes(results + [FLAT, FLAT]),
        in_specs=[HBM] * len(UPPER_IN),
        out_specs=[HBM] * 4,
        scratch_shapes=dma(len(UPPER_IN))
        + scratch(results + [((2, ROWS, PAIR), BF16)] + UPPER_IN + [wide, wide, narrow, narrow, TABLE, ((2, 32, PAIR), F32)] + sums),
        compiler_params=limited(60),
        name="upper",
    )(*args)


def body(region, cotangent, gains, qkv, qkv_bias, table, proj, up, up_bias, down):
    rows, cols = lax.axis_size("row"), lax.axis_size(COL_AXES)
    table_t = jnp.transpose(table, (1, 0, 2))
    down_t = jnp.transpose(down, (0, 2, 1))
    params = (gains, qkv_bias, table_t, up_bias, qkv, proj, up, down_t)
    low, send_a, send_b, *saved = run_lower(region, cotangent, *params)
    row_got = swap((send_a, send_b), "row", rows)
    *prepared, m, slope = pl.pallas_call(
        prepare_kernel,
        out_shape=shapes(PREPARED + SAVES[EARLY:]),
        in_specs=[HBM] * 9,
        out_specs=[HBM] * 10,
        scratch_shapes=dma(10)
        + scratch([TABLE, SAVES[8]] + WEIGHTS + SMALL + PREPARED + SAVES[EARLY:]),
        compiler_params=limited(60),
        cost_estimate=pl.CostEstimate(flops=10**9, bytes_accessed=4 * 10**6, transcendentals=0),
        name="prepare",
    )(saved[8], *params)
    own = pl.pallas_call(
        own_kernel,
        out_shape=jax.ShapeDtypeStruct((2, 2, TH, 8, C), BF16),
        in_specs=[VMEM] * 2,
        out_specs=VMEM,
        compiler_params=limited(8),
        cost_estimate=pl.CostEstimate(flops=10**9, bytes_accessed=10**6, transcendentals=0),
        name="own_strips",
    )(low, cotangent)
    strip = ((24, 8, C), BF16)
    send = pl.pallas_call(
        strip_kernel,
        out_shape=shapes([strip, strip]),
        in_specs=[VMEM] * 3,
        out_specs=[VMEM] * 2,
        compiler_params=limited(8),
        name="strips",
    )(own, *row_got)
    col_got = swap(send, COL_AXES, cols)
    out, grad_region, keep, give = run_upper(
        rows, cols, low, cotangent, *row_got, *col_got, qkv, proj, up, down_t, *prepared, *saved, m, slope
    )
    got = lax.ppermute(give, "core", near(2))
    share = (keep.astype(F32) + got.astype(F32)).astype(BF16).reshape(PEERS, -1, PAIR)
    peers = ("row", "col_half")
    parts = lax.all_to_all(share, peers, 0, 0)
    part = jnp.sum(parts.astype(F32), 0, keepdims=True).astype(BF16)
    mine = lax.all_to_all(jnp.broadcast_to(part, share.shape), peers, 0, 0)
    mine = mine.reshape(ROWS, PAIR)
    other = lax.ppermute(mine, "core", near(2))
    grads = pl.pallas_call(
        unpack_kernel,
        out_shape=tuple(
            jax.ShapeDtypeStruct(shape, F32)
            for shape in (
                (2, 2, C),
                (2, C, 3 * C),
                (2, 3 * C),
                (HEADS, 2, 225),
                (2, C, C),
                (2, C, HID),
                (2, HID),
                (2, C, HID),
            )
        ),
        in_specs=[VMEM] * 2,
        out_specs=[VMEM] * 8,
        compiler_params=limited(8),
        name="unpack",
    )(mine, other)
    d_gains, d_qkv, d_qkv_bias, d_table, d_proj, d_up, d_up_bias, d_down_t = grads
    return (
        out,
        grad_region,
        d_gains,
        d_qkv,
        d_qkv_bias,
        jnp.transpose(d_table, (1, 0, 2)),
        d_proj,
        d_up,
        d_up_bias,
        jnp.transpose(d_down_t, (0, 2, 1)),
    )


def solution(mesh):
    rows, cols = mesh.devices.shape
    fine = Mesh(mesh.devices.reshape(rows, cols // 2, 2), ("row", "col_half", "core"))
    tile = P("row", ("col_half", "core"), None)
    return jax.shard_map(
        body,
        mesh=fine,
        in_specs=(tile, tile) + (P(),) * 8,
        out_specs=(tile, tile) + (P(),) * 8,
        check_vma=False,
    )
```
